256 devices in a mesh: seq: 16 (over z, core), grp: 8 (over y_lo, x), tp: 2 (over y_hi).
Axes of the slice: x: 4, y: 4 (y_hi: 2, y_lo: 2; y = y_hi * 2 + y_lo), z: 8, core: 2. Of those that a mesh axis runs over, the one named last changes fastest.
Arguments:
- prefix_query: bfloat16 [8192, 8192], P('seq', ('grp', 'tp')), may hold values from -160 to 160
- prefix_key: bfloat16 [8192, 1024], P(('seq', 'tp'), 'grp'), may hold values from -6 to 6
- prefix_value: bfloat16 [8192, 1024], P(('seq', 'tp'), 'grp'), may hold values from -6 to 6
- step_query: bfloat16 [512, 4, 8192], P(('seq', 'grp', 'tp')), may hold values from -160 to 160
- cache_key: bfloat16 [512, 512, 1024], P(('seq', 'grp', 'tp')), may hold values from -6 to 6
- cache_value: bfloat16 [512, 512, 1024], P(('seq', 'grp', 'tp')), may hold values from -6 to 6
- step_key: bfloat16 [512, 4, 1024], P(('seq', 'grp', 'tp')), may hold values from -6 to 6
- step_value: bfloat16 [512, 4, 1024], P(('seq', 'grp', 'tp')), may hold values from -6 to 6
- suffix_lengths: int32 [512], P(('seq', 'grp', 'tp')), may hold values from 1 to 512, as said below
Outputs:
- prefix_output: bfloat16 [8192, 8192], P('seq', ('grp', 'tp'))
- step_output: bfloat16 [512, 4, 8192], P(('seq', 'grp', 'tp'))
The draws below stay inside these ranges and needn't reach their ends.
Inputs may be any that keep to these rules, and one draw needn't show every extreme that they name: `suffix_lengths`: some row has 512 live positions and some row has 1.
All inputs are finite; a program needn't handle non-finite values.
Results may differ from the reference program's by a relative error of at most 0.00595.
Values may be sent and summed in bfloat16 or wider, within the bound.
No kernel may reach another device: no remote copies, remote signals or barrier semaphores. Data moves between devices by JAX's collectives and lax.ppermute only.
A program may use at most 128 MiB of HBM per device.

```python
import math
import jax
import jax.numpy as jnp
from jax import lax

HEADS = 64
KV_HEADS = 8
HEAD_DIM = 128
STEPS = 4
SUFFIX = 512
PREFIX = 8192
ROWS = 512


def shared_prefix_keys(key):
    folded = jax.random.fold_in(key, 101)
    return jnp.clip(jax.random.normal(folded, (PREFIX, KV_HEADS * HEAD_DIM), jnp.float32), -6.0, 6.0)


def shared_step_keys(key):
    folded = jax.random.fold_in(key, 202)
    return jnp.clip(jax.random.normal(folded, (ROWS, STEPS, KV_HEADS * HEAD_DIM), jnp.float32), -6.0, 6.0)


def draw_prefix_query(key, part):
    key = jax.random.fold_in(key, 11)
    return jnp.clip(2.5 * jax.random.normal(key, (PREFIX, HEADS * HEAD_DIM), jnp.float32), -15.0, 15.0).astype(jnp.bfloat16)


def draw_prefix_key(key, part):
    return shared_prefix_keys(key).astype(jnp.bfloat16)


def draw_step_query(key, part):
    key = jax.random.fold_in(key, 13)
    return jnp.clip(2.5 * jax.random.normal(key, (ROWS, STEPS, HEADS * HEAD_DIM), jnp.float32), -15.0, 15.0).astype(jnp.bfloat16)


def draw_step_key(key, part):
    return shared_step_keys(key).astype(jnp.bfloat16)


def draw_suffix_lengths(key, part):
    key = jax.random.fold_in(key, 7)
    length_key, first_key, second_key = jax.random.split(key, 3)
    lengths = jax.random.randint(length_key, (ROWS,), 1, SUFFIX + 1)
    first_row = jax.random.randint(first_key, (), 0, ROWS)
    second_row = (first_row + 1 + jax.random.randint(second_key, (), 0, ROWS - 1)) % ROWS
    return lengths.at[first_row].set(SUFFIX).at[second_row].set(1).astype(jnp.int32)


def block_scale(stream_key, extent, cuts, smallest, largest):
    def one(position, parts):
        heights = jax.random.uniform(jax.random.fold_in(jax.random.fold_in(stream_key, 6), position), (parts,), jnp.float32, smallest / len(cuts), largest / len(cuts))
        return jnp.repeat(jnp.exp(heights), extent[position] // parts).reshape((-1,) + (1,) * (len(extent) - position - 1))

    gain = one(*cuts[0])
    for cut in cuts[1:]:
        gain = gain * one(*cut)
    return gain


def centred(key, shape, width, reach, cuts=(), held_as=jnp.bfloat16):
    drawn = width * jax.random.normal(key, shape, jnp.float32)
    if cuts:
        drawn = drawn * block_scale(key, shape, cuts, -0.22, 0.18)
    return jnp.clip(drawn, -reach, reach).astype(held_as)


def setup_inputs(seed: int = 0) -> dict:
    key_list = jax.random.split(jax.random.key(seed), 10)
    return {
        "prefix_query": draw_prefix_query(jax.random.fold_in(key_list[9], 71), 0),
        "prefix_key": draw_prefix_key(jax.random.fold_in(key_list[9], 71), 0),
        "prefix_value": centred(key_list[2], (PREFIX, KV_HEADS * HEAD_DIM), 1.0, 6.0, ((0, 32), (1, 8))),
        "step_query": draw_step_query(jax.random.fold_in(key_list[9], 71), 0),
        "cache_key": centred(key_list[4], (ROWS, SUFFIX, KV_HEADS * HEAD_DIM), 1.0, 6.0, ((0, 256),)),
        "cache_value": centred(key_list[5], (ROWS, SUFFIX, KV_HEADS * HEAD_DIM), 1.0, 6.0, ((0, 256),)),
        "step_key": draw_step_key(jax.random.fold_in(key_list[9], 71), 0),
        "step_value": centred(key_list[7], (ROWS, STEPS, KV_HEADS * HEAD_DIM), 1.0, 6.0, ((0, 256),)),
        "suffix_lengths": draw_suffix_lengths(jax.random.fold_in(key_list[9], 71), 0),
    }


NEGATIVE = -1e30
PRECISE = lax.Precision.HIGHEST


def softmax_apply(scores, allowed, values, form):
    scores = jnp.where(allowed, scores, NEGATIVE)
    highest = jnp.max(scores, axis=-1, keepdims=True)
    weights = jnp.where(allowed, jnp.exp(scores - highest), 0.0)
    totals = jnp.sum(weights, axis=-1)
    rounded = lax.optimization_barrier(weights.astype(jnp.bfloat16)).astype(jnp.float32)
    mixed_values = jnp.einsum(form, rounded, values, precision=PRECISE)
    return mixed_values, totals


def reference(prefix_query, prefix_key, prefix_value, step_query, cache_key, cache_value, step_key, step_value, suffix_lengths):
    group_size = HEADS // KV_HEADS
    score_scale = HEAD_DIM ** -0.5
    key_all = prefix_key.astype(jnp.float32).reshape(PREFIX, KV_HEADS, HEAD_DIM)
    value_all = prefix_value.astype(jnp.float32).reshape(PREFIX, KV_HEADS, HEAD_DIM)
    query_all = prefix_query.astype(jnp.float32).reshape(PREFIX, KV_HEADS, group_size, HEAD_DIM)
    block_rows = math.gcd(PREFIX, 512)
    pieces = []
    for block_index in range(PREFIX // block_rows):
        block_begin = block_index * block_rows
        finish = block_begin + block_rows
        query_pos = block_begin + jnp.arange(block_rows, dtype=jnp.int32)
        key_pos = jnp.arange(finish, dtype=jnp.int32)
        allowed = (key_pos[None, :] <= query_pos[:, None])[:, None, :]

        def one_head(operands):
            head_query, head_key, head_value = operands
            scores = jnp.einsum("qgd,nd->qgn", head_query, head_key, precision=PRECISE) * score_scale
            mixed_values, totals = softmax_apply(scores, allowed, head_value, "qgn,nd->qgd")
            return mixed_values / totals[..., None]

        outputs = lax.map(one_head, (jnp.moveaxis(query_all[block_begin:finish], 1, 0), jnp.moveaxis(key_all[:finish], 1, 0), jnp.moveaxis(value_all[:finish], 1, 0)))
        pieces.append(jnp.moveaxis(outputs, 0, 1).reshape(block_rows, HEADS * HEAD_DIM).astype(jnp.bfloat16))
    prefix_output = jnp.concatenate(pieces, axis=0)

    step_index = jnp.arange(STEPS, dtype=jnp.int32)
    fresh_allowed = step_index[None, :] <= step_index[:, None]
    prefix_allowed = jnp.zeros((STEPS, PREFIX), jnp.int32) == 0

    def one_row(operands):
        row_query, row_cache_key, row_cache_value, row_step_key, row_step_value, row_length = operands
        queries = row_query.astype(jnp.float32).reshape(STEPS, KV_HEADS, group_size, HEAD_DIM)
        row_keys = jnp.concatenate([key_all, row_cache_key.astype(jnp.float32).reshape(SUFFIX, KV_HEADS, HEAD_DIM), row_step_key.astype(jnp.float32).reshape(STEPS, KV_HEADS, HEAD_DIM)], axis=0)
        values = jnp.concatenate([value_all, row_cache_value.astype(jnp.float32).reshape(SUFFIX, KV_HEADS, HEAD_DIM), row_step_value.astype(jnp.float32).reshape(STEPS, KV_HEADS, HEAD_DIM)], axis=0)
        cache_allowed = jnp.arange(SUFFIX, dtype=jnp.int32) < row_length
        allowed = jnp.concatenate([prefix_allowed, jnp.broadcast_to(cache_allowed[None, :], (STEPS, SUFFIX)), fresh_allowed], axis=1)[:, None, None, :]
        scores = jnp.einsum("jkgd,nkd->jkgn", queries, row_keys, precision=PRECISE) * score_scale
        mixed_values, totals = softmax_apply(scores, allowed, values, "jkgn,nkd->jkgd")
        return (mixed_values / totals[..., None]).reshape(STEPS, HEADS * HEAD_DIM).astype(jnp.bfloat16)

    step_output = lax.map(one_row, (step_query, cache_key, cache_value, step_key, step_value, suffix_lengths))
    return prefix_output, step_output
```

```python
import functools

import jax
import jax.numpy as jnp
from jax import lax
from jax.experimental import pallas as pl
from jax.experimental.pallas import tpu as pltpu
from jax.sharding import PartitionSpec as P

HEADS = 64
KV_HEADS = 8
HEAD_DIM = 128
STEPS = 4
GROUP = HEADS // KV_HEADS

F32 = jnp.float32
BF16 = jnp.bfloat16
NEGATIVE = -1e30
SCALE = HEAD_DIM**-0.5 * 1.4426950408889634
LARGE = 2.0**100
NT = (((1,), (1,)), ((), ()))
NN = (((1,), (0,)), ((), ()))
EXT = HEAD_DIM + 16
LIMIT = 48 * 2**20
VM = pl.BlockSpec(memory_space=pltpu.VMEM)
SM = pl.BlockSpec(memory_space=pltpu.SMEM)


def dot(a, b, dims):
    return lax.dot_general(a, b, dims, preferred_element_type=F32)


def pack_kernel(key, value, out):
    out[0] = key[...]
    for tile in range(value.shape[0] // 128):
        rows = slice(tile * 128, (tile + 1) * 128)
        out[1, rows, :] = value[rows, :].astype(F32).T.astype(BF16)


def split3(x):
    high = x.astype(BF16).astype(F32)
    middle = (x - high).astype(BF16).astype(F32)
    return high, middle, (x - high - middle).astype(BF16).astype(F32)


def step_kernel(
    first, prefill, decode, last, widths, meta, *refs
):
    refs = list(refs)
    pieces = [refs.pop(0) for _ in widths]
    pq = refs.pop(0) if prefill else None
    dq = refs.pop(0) if decode else None
    heads = pq.shape[1] // HEAD_DIM if prefill else 0
    tiles = heads + (1 if decode else 0)
    if first:
        acc_in = c_in = None
    else:
        acc_in, c_in = refs.pop(0), refs.pop(0)
    if last:
        out_p = refs.pop(0) if prefill else None
        out_d = refs.pop(0) if decode else None
        acc_out = c_out = None
    else:
        acc_out, c_out = refs.pop(0), refs.pop(0)
    qs = refs.pop(0)
    vts = [refs.pop(0) for _ in widths]
    if last:
        acc_out, c_out = refs.pop(0), refs.pop(0)
    if first:
        acc_in, c_in = refs.pop(0), refs.pop(0)

    for head in range(heads):
        qs[head] = pq[:, head * HEAD_DIM : (head + 1) * HEAD_DIM]
    if decode:
        rows = dq.shape[0]
        for head in range(GROUP):
            qs[heads, head * rows : (head + 1) * rows, :] = dq[:, head * HEAD_DIM : (head + 1) * HEAD_DIM]
    for piece, vt in zip(pieces, vts):
        for half in range(piece.shape[0]):
            for tile in range(4):
                at = (half * 4 + tile) * 128
                vt[0:HEAD_DIM, at : at + 128] = piece[half, 1, tile * 128 : (tile + 1) * 128, :]
        vt[HEAD_DIM:EXT, :] = jnp.ones((EXT - HEAD_DIM, vt.shape[1]), BF16)

    def add(tile, number, init):
        piece, vt = pieces[number], vts[number]
        parts = [
            jnp.exp2(dot(piece[half, 0], qs[tile], NT) * SCALE - c_in[tile, 0:1, :]).astype(BF16)
            for half in range(piece.shape[0])
        ]
        weights = parts[0] if len(parts) == 1 else jnp.concatenate(parts, axis=0)
        return init + dot(vt[...], weights, NN)

    if first:
        own = meta[0]
        shape = (512, 512)
        row = lax.broadcasted_iota(jnp.int32, shape, 0)
        column = lax.broadcasted_iota(jnp.int32, shape, 1)
        position = jnp.where(row < 256, row + 256 * own, row - 256 * own)
        allowed = position <= column
        for tile in range(tiles):
            scores = dot(pieces[0][0, 0], qs[tile], NT) * SCALE
            if tile < heads:
                scores = jnp.where(allowed, scores, NEGATIVE)
            peak = jnp.max(scores, axis=0, keepdims=True)
            acc_in[tile] = dot(vts[0][...], jnp.exp2(scores - peak).astype(BF16), NN)
            c_in[tile] = jnp.broadcast_to(peak, c_in.shape[1:])
        rest = [1]
    else:
        rest = list(range(len(pieces)))

    acc_out[...] = acc_in[...]
    c_out[...] = c_in[...]
    for number in rest:
        if heads:

            @pl.when(meta[1 + number] > 0)
            def _():
                for tile in range(heads):
                    acc_out[tile] = add(tile, number, acc_out[tile])

    if decode:
        sums = acc_out[heads]
        for number in rest:
            sums = add(heads, number, sums)
        acc_out[heads] = sums

    top = jnp.max(acc_out[:, HEAD_DIM : HEAD_DIM + 1, :])

    @pl.when(jnp.logical_not(top < LARGE))
    def _():
        def again(tile, carry):
            acc_out[tile] = acc_in[tile]
            c_out[tile] = c_in[tile]
            for number in rest:

                @pl.when(jnp.logical_or(tile >= heads, meta[1 + number] > 0))
                def _():
                    for half in range(pieces[number].shape[0]):
                        scores = dot(pieces[number][half, 0], qs[tile], NT) * SCALE
                        before = c_out[tile, 0:1, :]
                        peak = jnp.maximum(before, jnp.max(scores, axis=0, keepdims=True))
                        update = dot(
                            vts[number][:, half * 512 : (half + 1) * 512],
                            jnp.exp2(scores - peak).astype(BF16),
                            NN,
                        )
                        acc_out[tile] = acc_out[tile] * jnp.exp2(before - peak) + update
                        c_out[tile] = jnp.broadcast_to(peak, c_out.shape[1:])

            return carry

        lax.fori_loop(0, tiles, again, 0)

    if last and prefill:
        for head in range(heads):
            totals = acc_out[head, HEAD_DIM : HEAD_DIM + 1, :]
            result = acc_out[head, 0:HEAD_DIM, :] * (1.0 / totals)
            out_p[:, head * HEAD_DIM : (head + 1) * HEAD_DIM] = result.T.astype(BF16)
    if last and decode:
        totals = acc_out[heads, HEAD_DIM : HEAD_DIM + 1, :]
        result = (acc_out[heads, 0:HEAD_DIM, :] * (1.0 / totals)).T.astype(BF16)
        rows = dq.shape[0]
        stats = list(split3(c_out[heads, 0:1, :])) + list(split3(totals))
        slot = lax.broadcasted_iota(jnp.int32, (HEAD_DIM, GROUP * rows), 0)
        column = lax.broadcasted_iota(jnp.int32, (HEAD_DIM, GROUP * rows), 1)
        table = jnp.zeros((HEAD_DIM, GROUP * rows), F32)
        for number, stat in enumerate(stats):
            table = jnp.where(slot % 16 == number, stat, table)
        table = jnp.where(slot // 16 == column // rows, table, 0.0).T
        packed = jnp.zeros((rows, HEAD_DIM), F32)
        for head in range(GROUP):
            out_d[:, head * HEAD_DIM : (head + 1) * HEAD_DIM] = result[head * rows : (head + 1) * rows, :]
            packed = packed + table[head * rows : (head + 1) * rows, :]
        out_d[:, GROUP * HEAD_DIM :] = packed.astype(BF16)


def step(meta, pieces, pq, dq, state, last=False):
    first = state is None and not last
    first = state is None
    prefill, decode = pq is not None, dq is not None
    heads = pq.shape[1] // HEAD_DIM if prefill else 0
    tiles = heads + (1 if decode else 0)
    queries = 512
    widths = tuple(512 * piece.shape[0] for piece in pieces)
    acc = (tiles, EXT, queries)
    cs = (tiles, 8, queries)
    args = [meta] + list(pieces) + [x for x in (pq, dq) if x is not None]
    if not first:
        args += list(state)
    if last:
        out_shape = []
        if prefill:
            out_shape.append(jax.ShapeDtypeStruct(pq.shape, BF16))
        if decode:
            out_shape.append(jax.ShapeDtypeStruct((dq.shape[0], dq.shape[1] + 128), BF16))
    else:
        out_shape = [jax.ShapeDtypeStruct(acc, F32), jax.ShapeDtypeStruct(cs, F32)]
    scratch = [pltpu.VMEM((tiles, queries, HEAD_DIM), BF16)]
    scratch += [pltpu.VMEM((EXT, width), BF16) for width in widths]
    if last:
        scratch += [pltpu.VMEM(acc, F32), pltpu.VMEM(cs, F32)]
    if first:
        scratch += [pltpu.VMEM(acc, F32), pltpu.VMEM(cs, F32)]
    flops = 4 * HEAD_DIM * tiles * queries * sum(widths)
    return pl.pallas_call(
        functools.partial(step_kernel, first, prefill, decode, last, widths),
        out_shape=out_shape,
        in_specs=[SM] + [VM] * (len(args) - 1),
        out_specs=[VM] * len(out_shape),
        scratch_shapes=scratch,
        compiler_params=pltpu.CompilerParams(vmem_limit_bytes=LIMIT),
        cost_estimate=pl.CostEstimate(
            flops=2 * flops, bytes_accessed=4 * 2**20, transcendentals=tiles * queries * sum(widths)
        ),
        name="step",
    )(*args)


def suffix_kernel(lengths, query, cache_key, cache_value, step_key, step_value, sums, peaks, totals):
    rows = cache_key.shape[0]
    positions = cache_key.shape[1]
    count = rows * STEPS
    queries = jnp.concatenate(
        [query[:, head * HEAD_DIM : (head + 1) * HEAD_DIM].astype(F32) for head in range(GROUP)], axis=0
    ).astype(BF16)

    def filled(fresh):
        return jnp.concatenate(
            [fresh[...].astype(F32), jnp.zeros((128 - count, HEAD_DIM), F32)], axis=0
        ).astype(BF16)

    shape = (GROUP * count, positions)
    place = lax.broadcasted_iota(jnp.int32, shape, 0) % count
    key_pos = lax.broadcasted_iota(jnp.int32, shape, 1)
    scores = []
    for row in range(rows):
        allowed = jnp.logical_and(place // STEPS == row, key_pos < lengths[row])
        scores.append(jnp.where(allowed, dot(queries, cache_key[row], NT) * SCALE, NEGATIVE))
    shape = (GROUP * count, 128)
    place = lax.broadcasted_iota(jnp.int32, shape, 0) % count
    fresh = lax.broadcasted_iota(jnp.int32, shape, 1)
    allowed = jnp.logical_and(place // STEPS == fresh // STEPS, fresh <= place)
    scores.append(jnp.where(allowed, dot(queries, filled(step_key), NT) * SCALE, NEGATIVE))
    peak = functools.reduce(jnp.maximum, [jnp.max(part, axis=1, keepdims=True) for part in scores])
    weights = [jnp.exp2(part - peak) for part in scores]
    total = functools.reduce(jnp.add, [jnp.sum(part, axis=1, keepdims=True) for part in weights])
    values = [cache_value[row] for row in range(rows)] + [filled(step_value)]
    result = dot(weights[0].astype(BF16), values[0], NN)
    for part, value in zip(weights[1:], values[1:]):
        result = result + dot(part.astype(BF16), value, NN)
    sums[0] = result
    peaks[0] = jnp.broadcast_to(peak, peaks.shape[1:])
    totals[0] = jnp.broadcast_to(total, totals.shape[1:])


def suffix(lengths, query, cache_key, cache_value, step_key, step_value):
    rows, positions, _ = cache_key.shape
    count = rows * STEPS
    out = jax.ShapeDtypeStruct((KV_HEADS, GROUP * count, HEAD_DIM), F32)
    cache_spec = pl.BlockSpec((rows, positions, HEAD_DIM), lambda c: (0, 0, c))
    fresh_spec = pl.BlockSpec((count, HEAD_DIM), lambda c: (0, c))
    out_spec = pl.BlockSpec((1, GROUP * count, HEAD_DIM), lambda c: (c, 0, 0))
    return pl.pallas_call(
        suffix_kernel,
        out_shape=[out] * 3,
        grid=(KV_HEADS,),
        in_specs=[
            SM,
            pl.BlockSpec((count, GROUP * HEAD_DIM), lambda c: (0, c)),
            cache_spec,
            cache_spec,
            fresh_spec,
            fresh_spec,
        ],
        out_specs=[out_spec] * 3,
        compiler_params=pltpu.CompilerParams(vmem_limit_bytes=LIMIT),
        cost_estimate=pl.CostEstimate(flops=3 * 10**9, bytes_accessed=6 * 2**20, transcendentals=10**6),
        name="suffix",
    )(
        lengths,
        query,
        cache_key,
        cache_value,
        step_key.reshape(count, -1),
        step_value.reshape(count, -1),
    )


def merge_kernel(prefix, sums, peaks, totals, out):
    count = out.shape[0]
    for kv in range(KV_HEADS):
        for head in range(GROUP):
            rows = slice(head * count, (head + 1) * count)
            lanes = slice(head * HEAD_DIM, (head + 1) * HEAD_DIM)
            at = GROUP * HEAD_DIM + 16 * head
            stats = prefix[kv, :, at : at + 6].astype(F32)
            c = stats[:, 0:1] + stats[:, 1:2] + stats[:, 2:3]
            total = stats[:, 3:4] + stats[:, 4:5] + stats[:, 5:6]
            peak = peaks[kv, rows, :]
            top = jnp.maximum(peak, c)
            prior = jnp.exp2(c - top) * total
            later = jnp.exp2(peak - top)
            mixed = prefix[kv, :, lanes].astype(F32) * prior + sums[kv, rows, :] * later
            mixed = mixed / (prior + totals[kv, rows, :] * later)
            at = (kv * GROUP + head) * HEAD_DIM
            out[:, at : at + HEAD_DIM] = mixed.astype(BF16)


def local(
    prefix_query,
    prefix_key,
    prefix_value,
    step_query,
    cache_key,
    cache_value,
    step_key,
    step_value,
    suffix_lengths,
):
    seq = lax.axis_index("seq")
    own_tp = lax.axis_index("tp")
    seq_count = lax.axis_size("seq")
    z, core = seq // 2, seq % 2
    ring = seq_count // 2

    def swap_cores(x):
        return lax.ppermute(x, "seq", [(i, i ^ 1) for i in range(seq_count)])

    def along_ring(x):
        return lax.ppermute(
            x, "seq", [(i, (i + (2 if i % 2 == 0 else -2)) % seq_count) for i in range(seq_count)]
        )

    count = step_query.shape[0] * STEPS
    flat_query = step_query.reshape(count, -1)

    own = pl.pallas_call(
        pack_kernel,
        out_shape=jax.ShapeDtypeStruct((2,) + prefix_key.shape, BF16),
        in_specs=[VM, VM],
        out_specs=VM,
        name="pack",
    )(prefix_key, prefix_value)
    other = lax.ppermute(own, "tp", [(0, 1), (1, 0)])
    routed = lax.all_to_all(
        flat_query.reshape(count, KV_HEADS, -1).transpose(1, 0, 2), "grp", split_axis=0, concat_axis=0, tiled=True
    )
    routed = routed.reshape(KV_HEADS * count, -1)
    tail = suffix(suffix_lengths, flat_query, cache_key, cache_value, step_key, step_value)

    mine = jnp.concatenate([own, other], axis=1)[None]
    theirs = swap_cores(mine)
    block = jnp.concatenate([mine, theirs], axis=0)

    received = []
    for hop in range(1, 5):
        block = along_ring(block if hop < 4 else block[0:1])
        received.append((block, swap_cores(block)))

    def flags(hop):
        mine_z = jnp.where(core == 0, z - hop, z + hop) % ring
        their_z = jnp.where(core == 0, z + hop, z - hop) % ring
        return [(mine_z < z).astype(jnp.int32), (their_z < z).astype(jnp.int32)]

    def meta(hop):
        values = [own_tp, jnp.int32(0), core] if hop == 0 else [own_tp] + flags(hop)
        return jnp.stack([jnp.asarray(value, jnp.int32) for value in values])

    state = step(meta(0), [mine, theirs], prefix_query, routed, None)
    for hop in range(1, 4):
        state = step(meta(hop), received[hop - 1], prefix_query, routed, state)
    heads = prefix_query.shape[1] // HEAD_DIM
    acc, cs = state
    (partial,) = step(meta(4), received[3], None, routed, (acc[heads:], cs[heads:]), last=True)
    back = lax.all_to_all(
        partial.reshape(KV_HEADS, count, -1), "grp", split_axis=0, concat_axis=0, tiled=True
    )
    (prefix_output,) = step(meta(4), received[3], prefix_query, None, (acc[:heads], cs[:heads]), last=True)
    step_output = pl.pallas_call(
        merge_kernel,
        out_shape=jax.ShapeDtypeStruct(flat_query.shape, BF16),
        in_specs=[VM] * 4,
        out_specs=VM,
        name="merge",
    )(back, *tail)
    return prefix_output, step_output.reshape(step_query.shape)


def solution(mesh):
    rows = P(("seq", "grp", "tp"), None, None)
    return jax.shard_map(
        local,
        mesh=mesh,
        in_specs=(
            P("seq", ("grp", "tp")),
            P(("seq", "tp"), "grp"),
            P(("seq", "tp"), "grp"),
            rows,
            rows,
            rows,
            rows,
            rows,
            P(("seq", "grp", "tp")),
        ),
        out_specs=(P("seq", ("grp", "tp")), rows),
        check_vma=False,
    )
```

```python
import functools

import jax
import jax.numpy as jnp
from jax import lax
from jax.experimental import pallas as pl
from jax.experimental.pallas import tpu as pltpu
from jax.sharding import PartitionSpec as P

HEADS = 64
KV_HEADS = 8
HEAD_DIM = 128
STEPS = 4
GROUP = HEADS // KV_HEADS

F32 = jnp.float32
BF16 = jnp.bfloat16
NEGATIVE = -1e30
SCALE = HEAD_DIM**-0.5 * 1.4426950408889634
LARGE = 2.0**100
NT = (((1,), (1,)), ((), ()))
NN = (((1,), (0,)), ((), ()))
EXT = HEAD_DIM + 16
LIMIT = 36 * 2**20
VM = pl.BlockSpec(memory_space=pltpu.VMEM)
SM = pl.BlockSpec(memory_space=pltpu.SMEM)
HBM = pl.BlockSpec(memory_space=pltpu.HBM)
CHUNKS = 4


def dot(a, b, dims):
    return lax.dot_general(a, b, dims, preferred_element_type=F32)


def pack_kernel(key, value, query, out, parts):
    out[0] = key[...]
    for tile in range(value.shape[0] // 128):
        rows = slice(tile * 128, (tile + 1) * 128)
        out[1, rows, :] = value[rows, :].astype(F32).T.astype(BF16)
    width = parts.shape[2]
    for kv in range(KV_HEADS):
        lanes = slice(kv * width, (kv + 1) * width)
        parts[kv] = jnp.concatenate(
            [query[row, :, lanes].astype(F32) for row in range(query.shape[0])], axis=0
        ).astype(BF16)


def stat_lanes(peak, total, count):
    lane = lax.broadcasted_iota(jnp.int32, (count, 128), 1)
    stats = jnp.zeros((count, 128), F32)
    for head in range(GROUP):
        here = slice(head * count, (head + 1) * count)
        for number, part in enumerate(split3(peak[here]) + split3(total[here])):
            stats = jnp.where(lane == 16 * head + number, part, stats)
    return stats.astype(BF16)


def split3(x):
    high = x.astype(BF16).astype(F32)
    middle = (x - high).astype(BF16).astype(F32)
    return high, middle, (x - high - middle).astype(BF16).astype(F32)


def step_kernel(first, prefill, decode, last, hops, early, meta, *refs):
    refs = list(refs)
    pieces = [refs.pop(0) for _ in range(len(hops) + early)]
    pq = refs.pop(0) if prefill else None
    dq = refs.pop(0) if decode else None
    if first:
        acc_in = c_in = None
    else:
        acc_in, c_in = refs.pop(0), refs.pop(0)
    if last:
        out_p = refs.pop(0) if prefill else None
        out_d = refs.pop(0) if decode else None
        acc_out = c_out = None
    else:
        acc_out, c_out = refs.pop(0), refs.pop(0)
    qs = refs.pop(0)
    vts = [refs.pop(0) for _ in pieces]
    if last:
        acc_out, c_out = refs.pop(0), refs.pop(0)
    if first:
        acc_in, c_in = refs.pop(0), refs.pop(0)
    decode_tile = acc_in.shape[0] - 1
    begin = 0 if prefill else decode_tile
    end = decode_tile + 1 if decode else decode_tile
    heads = range(begin, decode_tile)

    seq, own_tp = meta[0], meta[1]
    z, core = seq >> 1, seq & 1
    open_to_prefix = [core > 0 if hop == 0 else ((z - hop + 2 * hop * core) & 7) < z for hop in hops]

    for head in heads:
        qs[head] = pq[:, head * HEAD_DIM : (head + 1) * HEAD_DIM]
    if decode:
        rows = dq.shape[0]
        for head in range(GROUP):
            qs[decode_tile, head * rows : (head + 1) * rows, :] = dq[:, head * HEAD_DIM : (head + 1) * HEAD_DIM]
    for piece, vt in zip(pieces, vts):
        for half in range(piece.shape[0]):
            for tile in range(4):
                at = (half * 4 + tile) * 128
                vt[0:HEAD_DIM, at : at + 128] = piece[half, 1, tile * 128 : (tile + 1) * 128, :]
        vt[HEAD_DIM:EXT, :] = jnp.ones((EXT - HEAD_DIM, vt.shape[1]), BF16)

    def add(tile, number, init):
        piece, vt = pieces[number], vts[number]
        parts = [
            jnp.exp2(dot(piece[half, 0], qs[tile], NT) * SCALE - c_out[tile, 0:1, :]).astype(BF16)
            for half in range(piece.shape[0])
        ]
        weights = parts[0] if len(parts) == 1 else jnp.concatenate(parts, axis=0)
        return init + dot(vt[...], weights, NN)

    if first:
        shape = (512, 512)
        row = lax.broadcasted_iota(jnp.int32, shape, 0)
        column = lax.broadcasted_iota(jnp.int32, shape, 1)
        position = jnp.where(row < 256, row + 256 * own_tp, row - 256 * own_tp)
        allowed = position <= column
        for tile in heads:
            scores = jnp.where(allowed, dot(pieces[0][0, 0], qs[tile], NT) * SCALE, NEGATIVE)
            peak = jnp.max(scores, axis=0, keepdims=True)
            acc_in[tile] = dot(vts[0][...], jnp.exp2(scores - peak).astype(BF16), NN)
            c_in[tile] = jnp.broadcast_to(peak, c_in.shape[1:])
    rest = range(1 if first else 0, len(hops))

    copied = slice(begin, decode_tile if early else end)
    acc_out[copied] = acc_in[copied]
    c_out[copied] = c_in[copied]
    if early:
        scores = dot(pieces[len(hops)][0, 0], qs[decode_tile], NT) * SCALE
        peak = jnp.max(scores, axis=0, keepdims=True)
        c_out[decode_tile] = jnp.broadcast_to(peak, c_out.shape[1:])
        sums = dot(vts[len(hops)][...], jnp.exp2(scores - peak).astype(BF16), NN)
        for number in range(len(hops) + 1, len(pieces)):
            sums = add(decode_tile, number, sums)
        acc_out[decode_tile] = sums
    for number in rest:
        if prefill:

            @pl.when(open_to_prefix[number])
            def _():
                for tile in range(begin, end):
                    acc_out[tile] = add(tile, number, acc_out[tile])

        if decode:

            @pl.when(jnp.logical_not(open_to_prefix[number]) if prefill else number >= 0)
            def _():
                acc_out[decode_tile] = add(decode_tile, number, acc_out[decode_tile])

    top = jnp.max(acc_out[begin:end, HEAD_DIM : HEAD_DIM + 1, :])

    @pl.when(jnp.logical_not(top < LARGE))
    def _():
        def online(tile, number):
            for half in range(pieces[number].shape[0]):
                scores = dot(pieces[number][half, 0], qs[tile], NT) * SCALE
                before = c_out[tile, 0:1, :]
                peak = jnp.maximum(before, jnp.max(scores, axis=0, keepdims=True))
                update = dot(
                    vts[number][:, half * 512 : (half + 1) * 512], jnp.exp2(scores - peak).astype(BF16), NN
                )
                acc_out[tile] = acc_out[tile] * jnp.exp2(before - peak) + update
                c_out[tile] = jnp.broadcast_to(peak, c_out.shape[1:])

        def again(tile, carry):
            if early:

                @pl.when(tile == decode_tile)
                def _():
                    acc_out[tile] = jnp.zeros(acc_out.shape[1:], F32)
                    c_out[tile] = jnp.full(c_out.shape[1:], NEGATIVE, F32)
                    for number in range(len(hops), len(pieces)):
                        online(tile, number)

                @pl.when(tile < decode_tile)
                def _():
                    acc_out[tile] = acc_in[tile]
                    c_out[tile] = c_in[tile]

            else:
                acc_out[tile] = acc_in[tile]
                c_out[tile] = c_in[tile]
            for number in rest:

                @pl.when(jnp.logical_or(tile == decode_tile, open_to_prefix[number]))
                def _():
                    online(tile, number)

            return carry

        lax.fori_loop(begin, end, again, 0)

    if last and prefill:
        for head in heads:
            totals = acc_out[head, HEAD_DIM : HEAD_DIM + 1, :]
            result = (acc_out[head, 0:HEAD_DIM, :] * (1.0 / totals)).astype(BF16)
            out_p[:, head * HEAD_DIM : (head + 1) * HEAD_DIM] = result.T
    if last and decode:
        totals = acc_out[decode_tile, HEAD_DIM : HEAD_DIM + 1, :]
        result = (acc_out[decode_tile, 0:HEAD_DIM, :] * (1.0 / totals)).astype(BF16).T
        rows = dq.shape[0]
        stats = list(split3(c_out[decode_tile, 0:1, :])) + list(split3(totals))
        slot = lax.broadcasted_iota(jnp.int32, (HEAD_DIM, GROUP * rows), 0)
        column = lax.broadcasted_iota(jnp.int32, (HEAD_DIM, GROUP * rows), 1)
        table = jnp.zeros((HEAD_DIM, GROUP * rows), F32)
        for number, stat in enumerate(stats):
            table = jnp.where(slot % 16 == number, stat, table)
        table = jnp.where(slot // 16 == column // rows, table, 0.0).T
        packed = jnp.zeros((rows, HEAD_DIM), F32)
        for head in range(GROUP):
            out_d[:, head * HEAD_DIM : (head + 1) * HEAD_DIM] = result[head * rows : (head + 1) * rows, :]
            packed = packed + table[head * rows : (head + 1) * rows, :]
        out_d[:, GROUP * HEAD_DIM :] = packed.astype(BF16)


def step(meta, pieces, hops, pq, dq, state, last=False, early=()):
    first = state is None
    prefill, decode = pq is not None, dq is not None
    queries = 512
    tiles = 5 if first else state[0].shape[0]
    pieces = list(pieces) + list(early)
    widths = [512 * piece.shape[0] for piece in pieces]
    acc = (tiles, EXT, queries)
    cs = (tiles, 8, queries)
    args = [meta] + list(pieces) + [x for x in (pq, dq) if x is not None]
    if not first:
        args += list(state)
    if last:
        out_shape = []
        if prefill:
            out_shape.append(jax.ShapeDtypeStruct(pq.shape, BF16))
        if decode:
            out_shape.append(jax.ShapeDtypeStruct((dq.shape[0], dq.shape[1] + 128), BF16))
    else:
        out_shape = [jax.ShapeDtypeStruct(acc, F32), jax.ShapeDtypeStruct(cs, F32)]
    scratch = [pltpu.VMEM((tiles, queries, HEAD_DIM), BF16)]
    scratch += [pltpu.VMEM((EXT, width), BF16) for width in widths]
    if last or first:
        scratch += [pltpu.VMEM(acc, F32), pltpu.VMEM(cs, F32)]
    used = 4 * prefill + decode
    flops = 4 * HEAD_DIM * used * queries * sum(widths)
    return pl.pallas_call(
        functools.partial(step_kernel, first, prefill, decode, last, tuple(hops), len(early)),
        out_shape=out_shape,
        in_specs=[SM] + [VM] * (len(args) - 1),
        out_specs=[VM] * len(out_shape),
        scratch_shapes=scratch,
        compiler_params=pltpu.CompilerParams(vmem_limit_bytes=LIMIT),
        cost_estimate=pl.CostEstimate(
            flops=2 * flops, bytes_accessed=4 * 2**20, transcendentals=used * queries * sum(widths)
        ),
        name="step",
    )(*args)


def suffix_kernel(
    lengths, query, key_hbm, value_hbm, step_key, step_value, sums, stats, cache_key, cache_value, arrived
):
    rows, positions, lanes_all = cache_key.shape
    copies = []
    chunk = lanes_all // CHUNKS
    for number in range(CHUNKS):
        at = slice(number * chunk, (number + 1) * chunk)
        for which, (source, target) in enumerate(((key_hbm, cache_key), (value_hbm, cache_value))):
            copies.append(
                pltpu.make_async_copy(source.at[:, :, at], target.at[:, :, at], arrived.at[2 * number + which])
            )
    for copy in copies:
        copy.start()
    count = rows * STEPS
    shape = (GROUP * count, positions)
    place = lax.broadcasted_iota(jnp.int32, shape, 0) % count
    key_pos = lax.broadcasted_iota(jnp.int32, shape, 1)
    cached = [jnp.logical_and(place // STEPS == row, key_pos < lengths[row]) for row in range(rows)]
    shape = (GROUP * count, 128)
    place = lax.broadcasted_iota(jnp.int32, shape, 0) % count
    fresh = lax.broadcasted_iota(jnp.int32, shape, 1)
    recent = jnp.logical_and(place // STEPS == fresh // STEPS, fresh <= place)
    blank = jnp.zeros((128 - count, HEAD_DIM), F32)

    for kv in range(KV_HEADS):
        lanes = slice(kv * HEAD_DIM, (kv + 1) * HEAD_DIM)
        if kv % (KV_HEADS // CHUNKS) == 0:
            first = 2 * (kv // (KV_HEADS // CHUNKS))
            copies[first].wait()
            copies[first + 1].wait()
        queries = jnp.concatenate(
            [query[kv, :, head * HEAD_DIM : (head + 1) * HEAD_DIM].astype(F32) for head in range(GROUP)], axis=0
        ).astype(BF16)

        def filled(array):
            return jnp.concatenate(
                [array[row, :, lanes].astype(F32) for row in range(rows)] + [blank], axis=0
            ).astype(BF16)

        scores = [
            jnp.where(cached[row], dot(queries, cache_key[row, :, lanes], NT) * SCALE, NEGATIVE)
            for row in range(rows)
        ]
        scores.append(jnp.where(recent, dot(queries, filled(step_key), NT) * SCALE, NEGATIVE))
        peak = functools.reduce(jnp.maximum, [jnp.max(part, axis=1, keepdims=True) for part in scores])
        weights = [jnp.exp2(part - peak) for part in scores]
        total = functools.reduce(jnp.add, [jnp.sum(part, axis=1, keepdims=True) for part in weights])
        values = [cache_value[row, :, lanes] for row in range(rows)] + [filled(step_value)]
        result = dot(weights[0].astype(BF16), values[0], NN)
        for part, value in zip(weights[1:], values[1:]):
            result = result + dot(part.astype(BF16), value, NN)
        for head in range(GROUP):
            sums[kv, :, head * HEAD_DIM : (head + 1) * HEAD_DIM] = result[head * count : (head + 1) * count, :]
        stats[kv] = stat_lanes(peak, total, count)


def suffix(lengths, query, cache_key, cache_value, step_key, step_value):
    count = query.shape[1]
    return pl.pallas_call(
        suffix_kernel,
        out_shape=[
            jax.ShapeDtypeStruct(query.shape, F32),
            jax.ShapeDtypeStruct((KV_HEADS, count, 128), BF16),
        ],
        in_specs=[SM, VM, HBM, HBM, VM, VM],
        out_specs=[VM] * 2,
        scratch_shapes=[
            pltpu.VMEM(cache_key.shape, BF16),
            pltpu.VMEM(cache_value.shape, BF16),
            pltpu.SemaphoreType.DMA((2 * CHUNKS,)),
        ],
        compiler_params=pltpu.CompilerParams(vmem_limit_bytes=60 * 2**20),
        cost_estimate=pl.CostEstimate(flops=3 * 10**9, bytes_accessed=6 * 2**20, transcendentals=10**6),
        name="suffix",
    )(lengths, query, cache_key, cache_value, step_key, step_value)


def merge_kernel(prefix, sums, stats, out):
    width = GROUP * HEAD_DIM
    slot = lax.broadcasted_iota(jnp.int32, (128, width), 0)
    head = lax.broadcasted_iota(jnp.int32, (128, width), 1) // HEAD_DIM
    pick_c = jnp.where(jnp.logical_and(slot // 16 == head, slot % 16 < 3), 1.0, 0.0).astype(BF16)
    pick_total = jnp.where(
        jnp.logical_and(slot // 16 == head, jnp.logical_and(slot % 16 >= 3, slot % 16 < 6)), 1.0, 0.0
    ).astype(BF16)
    count = prefix.shape[1]
    early = jnp.concatenate([prefix[kv, :, width:].astype(F32) for kv in range(KV_HEADS)], axis=0).astype(BF16)
    late = jnp.concatenate([stats[kv].astype(F32) for kv in range(KV_HEADS)], axis=0).astype(BF16)
    c, total = dot(early, pick_c, NN), dot(early, pick_total, NN)
    peak, late_total = dot(late, pick_c, NN), dot(late, pick_total, NN)
    top = jnp.maximum(peak, c)
    prior = jnp.exp2(c - top) * total
    later = jnp.exp2(peak - top)
    scale = 1.0 / (prior + late_total * later)
    prior, later = prior * scale, later * scale
    for kv in range(KV_HEADS):
        rows = slice(kv * count, (kv + 1) * count)
        mixed = prefix[kv, :, 0:width].astype(F32) * prior[rows] + sums[kv] * later[rows]
        for row in range(out.shape[0]):
            out[row, :, kv * width : (kv + 1) * width] = mixed[row * STEPS : (row + 1) * STEPS].astype(BF16)


def local(
    prefix_query,
    prefix_key,
    prefix_value,
    step_query,
    cache_key,
    cache_value,
    step_key,
    step_value,
    suffix_lengths,
):
    meta = jnp.stack([lax.axis_index("seq"), lax.axis_index("tp")])
    seq_count = 16

    def swap_cores(x):
        return lax.ppermute(x, "seq", [(i, i ^ 1) for i in range(seq_count)])

    def along_ring(x):
        return lax.ppermute(
            x, "seq", [(i, (i + (2 if i % 2 == 0 else -2)) % seq_count) for i in range(seq_count)]
        )

    def over_groups(x):
        return lax.all_to_all(x, "grp", split_axis=0, concat_axis=0, tiled=True)

    count = step_query.shape[0] * STEPS
    width = GROUP * HEAD_DIM
    own, parts = pl.pallas_call(
        pack_kernel,
        out_shape=[
            jax.ShapeDtypeStruct((2,) + prefix_key.shape, BF16),
            jax.ShapeDtypeStruct((KV_HEADS, count, width), BF16),
        ],
        in_specs=[VM] * 3,
        out_specs=[VM] * 2,
        compiler_params=pltpu.CompilerParams(vmem_limit_bytes=60 * 2**20),
        name="pack",
    )(prefix_key, prefix_value, step_query)
    other = lax.ppermute(own, "tp", [(0, 1), (1, 0)])
    tail = suffix(suffix_lengths, parts, cache_key, cache_value, step_key, step_value)
    other, tail = lax.optimization_barrier((other, tail))

    mine = jnp.concatenate([own, other], axis=1)[None]
    theirs = swap_cores(mine)
    block = jnp.concatenate([mine, theirs], axis=0)

    coming = along_ring(block)
    parts, block = lax.optimization_barrier((parts, block))
    routed = over_groups(parts).reshape(KV_HEADS * count, width)
    state = step(meta, [mine, theirs], [0, 0], prefix_query, None, None)
    state, routed = lax.optimization_barrier((state, routed))
    block, state = lax.optimization_barrier((coming, state))
    for hop in range(1, 4):
        coming = along_ring(block)
        across = swap_cores(block)
        early = (mine, theirs) if hop == 1 else ()
        state = step(meta, [block, across], [hop, -hop], prefix_query, routed, state, early=early)
        block, state = lax.optimization_barrier((coming, state))
    (partial,) = step(meta, [block], [4], None, routed, state, last=True)
    back = over_groups(partial.reshape(KV_HEADS, count, -1))
    (prefix_output,) = step(meta, [block], [4], prefix_query, None, state, last=True)
    step_output = pl.pallas_call(
        merge_kernel,
        out_shape=jax.ShapeDtypeStruct(step_query.shape, BF16),
        in_specs=[VM] * 3,
        out_specs=VM,
        compiler_params=pltpu.CompilerParams(vmem_limit_bytes=24 * 2**20),
        name="merge",
    )(back, *tail)
    return prefix_output, step_output


def solution(mesh):
    rows = P(("seq", "grp", "tp"), None, None)
    return jax.shard_map(
        local,
        mesh=mesh,
        in_specs=(
            P("seq", ("grp", "tp")),
            P(("seq", "tp"), "grp"),
            P(("seq", "tp"), "grp"),
            rows,
            rows,
            rows,
            rows,
            rows,
            P(("seq", "grp", "tp")),
        ),
        out_specs=(P("seq", ("grp", "tp")), rows),
        check_vma=False,
    )
```

```python
import functools

import jax
import jax.numpy as jnp
from jax import lax
from jax.experimental import pallas as pl
from jax.experimental.pallas import tpu as pltpu
from jax.sharding import PartitionSpec as P

HEADS = 64
KV_HEADS = 8
HEAD_DIM = 128
STEPS = 4
GROUP = HEADS // KV_HEADS

F32 = jnp.float32
BF16 = jnp.bfloat16
NEGATIVE = -1e30
SCALE = HEAD_DIM**-0.5 * 1.4426950408889634
LARGE = 2.0**100
NT = (((1,), (1,)), ((), ()))
NN = (((1,), (0,)), ((), ()))
EXT = HEAD_DIM + 16
LIMIT = 36 * 2**20
VM = pl.BlockSpec(memory_space=pltpu.VMEM)
SM = pl.BlockSpec(memory_space=pltpu.SMEM)
HBM = pl.BlockSpec(memory_space=pltpu.HBM)
CHUNKS = 4


def dot(a, b, dims):
    return lax.dot_general(a, b, dims, preferred_element_type=F32)


def pack_kernel(key, value, query, out, parts):
    out[0] = key[...]
    for tile in range(value.shape[0] // 128):
        rows = slice(tile * 128, (tile + 1) * 128)
        out[1, rows, :] = value[rows, :].astype(F32).T.astype(BF16)
    width = parts.shape[2]
    for kv in range(KV_HEADS):
        lanes = slice(kv * width, (kv + 1) * width)
        parts[kv] = jnp.concatenate(
            [query[row, :, lanes].astype(F32) for row in range(query.shape[0])], axis=0
        ).astype(BF16)


def stat_lanes(peak, total, count):
    lane = lax.broadcasted_iota(jnp.int32, (count, 128), 1)
    stats = jnp.zeros((count, 128), F32)
    for head in range(GROUP):
        here = slice(head * count, (head + 1) * count)
        for number, part in enumerate(split3(peak[here]) + split3(total[here])):
            stats = jnp.where(lane == 16 * head + number, part, stats)
    return stats.astype(BF16)


def split3(x):
    high = x.astype(BF16).astype(F32)
    middle = (x - high).astype(BF16).astype(F32)
    return high, middle, (x - high - middle).astype(BF16).astype(F32)


def step_kernel(first, prefill, decode, last, hops, meta, *refs):
    refs = list(refs)
    pieces = [refs.pop(0) for _ in hops]
    pq = refs.pop(0) if prefill else None
    dq = refs.pop(0) if decode else None
    if first:
        acc_in = c_in = None
    else:
        acc_in, c_in = refs.pop(0), refs.pop(0)
    if last:
        out_p = refs.pop(0) if prefill else None
        out_d = refs.pop(0) if decode else None
        acc_out = c_out = None
    else:
        acc_out, c_out = refs.pop(0), refs.pop(0)
    qs = refs.pop(0)
    vts = [refs.pop(0) for _ in pieces]
    if last:
        acc_out, c_out = refs.pop(0), refs.pop(0)
    if first:
        acc_in, c_in = refs.pop(0), refs.pop(0)
    decode_tile = acc_in.shape[0] - 1
    begin = 0 if prefill else decode_tile
    end = decode_tile + 1 if decode else decode_tile
    heads = range(begin, decode_tile)

    seq, own_tp = meta[0], meta[1]
    z, core = seq >> 1, seq & 1
    open_to_prefix = [core > 0 if hop == 0 else ((z - hop + 2 * hop * core) & 7) < z for hop in hops]

    for head in heads:
        qs[head] = pq[:, head * HEAD_DIM : (head + 1) * HEAD_DIM]
    if decode:
        rows = dq.shape[0]
        for head in range(GROUP):
            qs[decode_tile, head * rows : (head + 1) * rows, :] = dq[:, head * HEAD_DIM : (head + 1) * HEAD_DIM]
    for piece, vt in zip(pieces, vts):
        for half in range(piece.shape[0]):
            for tile in range(4):
                at = (half * 4 + tile) * 128
                vt[0:HEAD_DIM, at : at + 128] = piece[half, 1, tile * 128 : (tile + 1) * 128, :]
        vt[HEAD_DIM:EXT, :] = jnp.ones((EXT - HEAD_DIM, vt.shape[1]), BF16)

    def add(tile, number, init):
        piece, vt = pieces[number], vts[number]
        parts = [
            jnp.exp2(dot(piece[half, 0], qs[tile], NT) * SCALE - c_out[tile, 0:1, :]).astype(BF16)
            for half in range(piece.shape[0])
        ]
        weights = parts[0] if len(parts) == 1 else jnp.concatenate(parts, axis=0)
        return init + dot(vt[...], weights, NN)

    if first:
        shape = (512, 512)
        row = lax.broadcasted_iota(jnp.int32, shape, 0)
        column = lax.broadcasted_iota(jnp.int32, shape, 1)
        position = jnp.where(row < 256, row + 256 * own_tp, row - 256 * own_tp)
        allowed = position <= column
        for tile in range(begin, end):
            scores = dot(pieces[0][0, 0], qs[tile], NT) * SCALE
            if tile in heads:
                scores = jnp.where(allowed, scores, NEGATIVE)
            peak = jnp.max(scores, axis=0, keepdims=True)
            acc_in[tile] = dot(vts[0][...], jnp.exp2(scores - peak).astype(BF16), NN)
            c_in[tile] = jnp.broadcast_to(peak, c_in.shape[1:])
    rest = range(1 if first else 0, len(hops))

    acc_out[begin:end] = acc_in[begin:end]
    c_out[begin:end] = c_in[begin:end]
    for number in rest:
        if prefill:

            @pl.when(open_to_prefix[number])
            def _():
                for tile in range(begin, end):
                    acc_out[tile] = add(tile, number, acc_out[tile])

        if decode:

            @pl.when(jnp.logical_not(open_to_prefix[number]) if prefill else number >= 0)
            def _():
                acc_out[decode_tile] = add(decode_tile, number, acc_out[decode_tile])

    top = jnp.max(acc_out[begin:end, HEAD_DIM : HEAD_DIM + 1, :])

    @pl.when(jnp.logical_not(top < LARGE))
    def _():
        def online(tile, number):
            piece, vt = pieces[number], vts[number]

            def some(part, carry):
                keys = piece[part // 4, 0, pl.ds(pl.multiple_of(part % 4 * 128, 128), 128), :]
                scores = dot(keys, qs[tile], NT) * SCALE
                before = c_out[tile, 0:1, :]
                peak = jnp.maximum(before, jnp.max(scores, axis=0, keepdims=True))
                values = vt[:, pl.ds(pl.multiple_of(part * 128, 128), 128)]
                update = dot(values, jnp.exp2(scores - peak).astype(BF16), NN)
                acc_out[tile] = acc_out[tile] * jnp.exp2(before - peak) + update
                c_out[tile] = jnp.broadcast_to(peak, c_out.shape[1:])
                return carry

            lax.fori_loop(0, vt.shape[1] // 128, some, 0)

        def again(tile, carry):
            acc_out[tile] = acc_in[tile]
            c_out[tile] = c_in[tile]
            for number in rest:

                @pl.when(jnp.logical_or(tile == decode_tile, open_to_prefix[number]))
                def _():
                    online(tile, number)

            return carry

        lax.fori_loop(begin, end, again, 0)

    if last and prefill:
        for head in heads:
            totals = acc_out[head, HEAD_DIM : HEAD_DIM + 1, :]
            result = (acc_out[head, 0:HEAD_DIM, :] * (1.0 / totals)).astype(BF16)
            out_p[:, head * HEAD_DIM : (head + 1) * HEAD_DIM] = result.T
    if last and decode:
        totals = acc_out[decode_tile, HEAD_DIM : HEAD_DIM + 1, :]
        result = (acc_out[decode_tile, 0:HEAD_DIM, :] * (1.0 / totals)).astype(BF16).T
        rows = dq.shape[0]
        stats = list(split3(c_out[decode_tile, 0:1, :])) + list(split3(totals))
        slot = lax.broadcasted_iota(jnp.int32, (HEAD_DIM, GROUP * rows), 0)
        column = lax.broadcasted_iota(jnp.int32, (HEAD_DIM, GROUP * rows), 1)
        table = jnp.zeros((HEAD_DIM, GROUP * rows), F32)
        for number, stat in enumerate(stats):
            table = jnp.where(slot % 16 == number, stat, table)
        table = jnp.where(slot // 16 == column // rows, table, 0.0).T
        packed = jnp.zeros((rows, HEAD_DIM), F32)
        for head in range(GROUP):
            out_d[:, head * HEAD_DIM : (head + 1) * HEAD_DIM] = result[head * rows : (head + 1) * rows, :]
            packed = packed + table[head * rows : (head + 1) * rows, :]
        out_d[:, GROUP * HEAD_DIM :] = packed.astype(BF16)


def step(meta, pieces, hops, pq, dq, state, last=False):
    first = state is None
    prefill, decode = pq is not None, dq is not None
    queries = 512
    tiles = 5 if first else state[0].shape[0]
    widths = [512 * piece.shape[0] for piece in pieces]
    acc = (tiles, EXT, queries)
    cs = (tiles, 8, queries)
    args = [meta] + list(pieces) + [x for x in (pq, dq) if x is not None]
    if not first:
        args += list(state)
    if last:
        out_shape = []
        if prefill:
            out_shape.append(jax.ShapeDtypeStruct(pq.shape, BF16))
        if decode:
            out_shape.append(jax.ShapeDtypeStruct((dq.shape[0], dq.shape[1] + 128), BF16))
    else:
        out_shape = [jax.ShapeDtypeStruct(acc, F32), jax.ShapeDtypeStruct(cs, F32)]
    scratch = [pltpu.VMEM((tiles, queries, HEAD_DIM), BF16)]
    scratch += [pltpu.VMEM((EXT, width), BF16) for width in widths]
    if last or first:
        scratch += [pltpu.VMEM(acc, F32), pltpu.VMEM(cs, F32)]
    used = 4 * prefill + decode
    flops = 4 * HEAD_DIM * used * queries * sum(widths)
    return pl.pallas_call(
        functools.partial(step_kernel, first, prefill, decode, last, tuple(hops)),
        out_shape=out_shape,
        in_specs=[SM] + [VM] * (len(args) - 1),
        out_specs=[VM] * len(out_shape),
        scratch_shapes=scratch,
        compiler_params=pltpu.CompilerParams(vmem_limit_bytes=LIMIT),
        cost_estimate=pl.CostEstimate(
            flops=2 * flops, bytes_accessed=4 * 2**20, transcendentals=used * queries * sum(widths)
        ),
        name="step",
    )(*args)


def suffix_kernel(
    lengths, query, key_hbm, value_hbm, step_key, step_value, sums, stats, cache_key, cache_value, arrived
):
    rows, positions, lanes_all = cache_key.shape
    copies = []
    chunk = lanes_all // CHUNKS
    for number in range(CHUNKS):
        at = slice(number * chunk, (number + 1) * chunk)
        for which, (source, target) in enumerate(((key_hbm, cache_key), (value_hbm, cache_value))):
            copies.append(
                pltpu.make_async_copy(source.at[:, :, at], target.at[:, :, at], arrived.at[2 * number + which])
            )
    for copy in copies:
        copy.start()
    count = rows * STEPS
    shape = (GROUP * count, positions)
    place = lax.broadcasted_iota(jnp.int32, shape, 0) % count
    key_pos = lax.broadcasted_iota(jnp.int32, shape, 1)
    cached = [jnp.logical_and(place // STEPS == row, key_pos < lengths[row]) for row in range(rows)]
    shape = (GROUP * count, 128)
    place = lax.broadcasted_iota(jnp.int32, shape, 0) % count
    fresh = lax.broadcasted_iota(jnp.int32, shape, 1)
    recent = jnp.logical_and(place // STEPS == fresh // STEPS, fresh <= place)
    blank = jnp.zeros((128 - count, HEAD_DIM), F32)

    for kv in range(KV_HEADS):
        lanes = slice(kv * HEAD_DIM, (kv + 1) * HEAD_DIM)
        if kv % (KV_HEADS // CHUNKS) == 0:
            first = 2 * (kv // (KV_HEADS // CHUNKS))
            copies[first].wait()
            copies[first + 1].wait()
        queries = jnp.concatenate(
            [query[kv, :, head * HEAD_DIM : (head + 1) * HEAD_DIM].astype(F32) for head in range(GROUP)], axis=0
        ).astype(BF16)

        def filled(array):
            return jnp.concatenate(
                [array[row, :, lanes].astype(F32) for row in range(rows)] + [blank], axis=0
            ).astype(BF16)

        scores = [
            jnp.where(cached[row], dot(queries, cache_key[row, :, lanes], NT) * SCALE, NEGATIVE)
            for row in range(rows)
        ]
        scores.append(jnp.where(recent, dot(queries, filled(step_key), NT) * SCALE, NEGATIVE))
        peak = functools.reduce(jnp.maximum, [jnp.max(part, axis=1, keepdims=True) for part in scores])
        weights = [jnp.exp2(part - peak) for part in scores]
        total = functools.reduce(jnp.add, [jnp.sum(part, axis=1, keepdims=True) for part in weights])
        values = [cache_value[row, :, lanes] for row in range(rows)] + [filled(step_value)]
        result = dot(weights[0].astype(BF16), values[0], NN)
        for part, value in zip(weights[1:], values[1:]):
            result = result + dot(part.astype(BF16), value, NN)
        for head in range(GROUP):
            sums[kv, :, head * HEAD_DIM : (head + 1) * HEAD_DIM] = result[head * count : (head + 1) * count, :]
        stats[kv] = stat_lanes(peak, total, count)


def suffix(lengths, query, cache_key, cache_value, step_key, step_value):
    count = query.shape[1]
    return pl.pallas_call(
        suffix_kernel,
        out_shape=[
            jax.ShapeDtypeStruct(query.shape, F32),
            jax.ShapeDtypeStruct((KV_HEADS, count, 128), BF16),
        ],
        in_specs=[SM, VM, HBM, HBM, VM, VM],
        out_specs=[VM] * 2,
        scratch_shapes=[
            pltpu.VMEM(cache_key.shape, BF16),
            pltpu.VMEM(cache_value.shape, BF16),
            pltpu.SemaphoreType.DMA((2 * CHUNKS,)),
        ],
        compiler_params=pltpu.CompilerParams(vmem_limit_bytes=60 * 2**20),
        cost_estimate=pl.CostEstimate(flops=3 * 10**9, bytes_accessed=6 * 2**20, transcendentals=10**6),
        name="suffix",
    )(lengths, query, cache_key, cache_value, step_key, step_value)


def merge_kernel(prefix, sums, stats, out):
    width = GROUP * HEAD_DIM
    slot = lax.broadcasted_iota(jnp.int32, (128, width), 0)
    head = lax.broadcasted_iota(jnp.int32, (128, width), 1) // HEAD_DIM
    pick_c = jnp.where(jnp.logical_and(slot // 16 == head, slot % 16 < 3), 1.0, 0.0).astype(BF16)
    pick_total = jnp.where(
        jnp.logical_and(slot // 16 == head, jnp.logical_and(slot % 16 >= 3, slot % 16 < 6)), 1.0, 0.0
    ).astype(BF16)
    count = prefix.shape[1]
    early = jnp.concatenate([prefix[kv, :, width:].astype(F32) for kv in range(KV_HEADS)], axis=0).astype(BF16)
    late = jnp.concatenate([stats[kv].astype(F32) for kv in range(KV_HEADS)], axis=0).astype(BF16)
    c, total = dot(early, pick_c, NN), dot(early, pick_total, NN)
    peak, late_total = dot(late, pick_c, NN), dot(late, pick_total, NN)
    top = jnp.maximum(peak, c)
    prior = jnp.exp2(c - top) * total
    later = jnp.exp2(peak - top)
    scale = 1.0 / (prior + late_total * later)
    prior, later = prior * scale, later * scale
    for kv in range(KV_HEADS):
        rows = slice(kv * count, (kv + 1) * count)
        mixed = prefix[kv, :, 0:width].astype(F32) * prior[rows] + sums[kv] * later[rows]
        for row in range(out.shape[0]):
            out[row, :, kv * width : (kv + 1) * width] = mixed[row * STEPS : (row + 1) * STEPS].astype(BF16)


def local(
    prefix_query,
    prefix_key,
    prefix_value,
    step_query,
    cache_key,
    cache_value,
    step_key,
    step_value,
    suffix_lengths,
):
    meta = jnp.stack([lax.axis_index("seq"), lax.axis_index("tp")])
    seq_count = 16

    def swap_cores(x):
        return lax.ppermute(x, "seq", [(i, i ^ 1) for i in range(seq_count)])

    def along_ring(x):
        return lax.ppermute(
            x, "seq", [(i, (i + (2 if i % 2 == 0 else -2)) % seq_count) for i in range(seq_count)]
        )

    def over_groups(x):
        return lax.all_to_all(x, "grp", split_axis=0, concat_axis=0, tiled=True)

    count = step_query.shape[0] * STEPS
    width = GROUP * HEAD_DIM
    own, parts = pl.pallas_call(
        pack_kernel,
        out_shape=[
            jax.ShapeDtypeStruct((2,) + prefix_key.shape, BF16),
            jax.ShapeDtypeStruct((KV_HEADS, count, width), BF16),
        ],
        in_specs=[VM] * 3,
        out_specs=[VM] * 2,
        compiler_params=pltpu.CompilerParams(vmem_limit_bytes=60 * 2**20),
        name="pack",
    )(prefix_key, prefix_value, step_query)
    other = lax.ppermute(own, "tp", [(0, 1), (1, 0)])
    tail = suffix(suffix_lengths, parts, cache_key, cache_value, step_key, step_value)
    other, tail = lax.optimization_barrier((other, tail))

    mine = jnp.concatenate([own, other], axis=1)[None]
    theirs = swap_cores(mine)
    block = jnp.concatenate([mine, theirs], axis=0)

    coming = along_ring(block)
    parts, block = lax.optimization_barrier((parts, block))
    routed = over_groups(parts)
    block, routed = lax.optimization_barrier((coming, routed))
    routed = routed.reshape(KV_HEADS * count, width)
    coming, across = along_ring(block), swap_cores(block)
    state = step(meta, [mine, theirs, block], [0, 0, 1], prefix_query, routed, None)
    for hop in range(2, 4):
        block, before, state = lax.optimization_barrier((coming, across, state))
        coming, across = along_ring(block), swap_cores(block)
        state = step(meta, [before, block], [1 - hop, hop], prefix_query, routed, state)
    before, state = lax.optimization_barrier((across, state))
    state = step(meta, [before], [-3], prefix_query, routed, state)
    block, state = lax.optimization_barrier((coming, state))
    (partial,) = step(meta, [block], [4], None, routed, state, last=True)
    back = over_groups(partial.reshape(KV_HEADS, count, -1))
    (prefix_output,) = step(meta, [block], [4], prefix_query, None, state, last=True)
    step_output = pl.pallas_call(
        merge_kernel,
        out_shape=jax.ShapeDtypeStruct(step_query.shape, BF16),
        in_specs=[VM] * 3,
        out_specs=VM,
        compiler_params=pltpu.CompilerParams(vmem_limit_bytes=24 * 2**20),
        name="merge",
    )(back, *tail)
    return prefix_output, step_output


def solution(mesh):
    rows = P(("seq", "grp", "tp"), None, None)
    return jax.shard_map(
        local,
        mesh=mesh,
        in_specs=(
            P("seq", ("grp", "tp")),
            P(("seq", "tp"), "grp"),
            P(("seq", "tp"), "grp"),
            rows,
            rows,
            rows,
            rows,
            rows,
            P(("seq", "grp", "tp")),
        ),
        out_specs=(P("seq", ("grp", "tp")), rows),
        check_vma=False,
    )
```

```python
import functools

import jax
import jax.numpy as jnp
from jax import lax
from jax.experimental import pallas as pl
from jax.experimental.pallas import tpu as pltpu
from jax.sharding import PartitionSpec as P

HEADS = 64
KV_HEADS = 8
HEAD_DIM = 128
STEPS = 4
GROUP = HEADS // KV_HEADS

F32 = jnp.float32
BF16 = jnp.bfloat16
NEGATIVE = -1e30
SCALE = HEAD_DIM**-0.5 * 1.4426950408889634
LARGE = 2.0**100
NT = (((1,), (1,)), ((), ()))
NN = (((1,), (0,)), ((), ()))
EXT = HEAD_DIM + 16
LIMIT = 36 * 2**20
VM = pl.BlockSpec(memory_space=pltpu.VMEM)
SM = pl.BlockSpec(memory_space=pltpu.SMEM)
HBM = pl.BlockSpec(memory_space=pltpu.HBM)
CHUNKS = 2


def dot(a, b, dims):
    return lax.dot_general(a, b, dims, preferred_element_type=F32)


def pack_kernel(key, value, query, out, parts):
    out[0] = key[...]
    for tile in range(value.shape[0] // 128):
        rows = slice(tile * 128, (tile + 1) * 128)
        out[1, rows, :] = value[rows, :].astype(F32).T.astype(BF16)
    width = parts.shape[2]
    for kv in range(KV_HEADS):
        lanes = slice(kv * width, (kv + 1) * width)
        parts[kv] = jnp.concatenate(
            [query[row, :, lanes].astype(F32) for row in range(query.shape[0])], axis=0
        ).astype(BF16)


def stat_lanes(peak, total, count):
    lane = lax.broadcasted_iota(jnp.int32, (count, 128), 1)
    stats = jnp.zeros((count, 128), F32)
    for head in range(GROUP):
        here = slice(head * count, (head + 1) * count)
        for number, part in enumerate(split3(peak[here]) + split3(total[here])):
            stats = jnp.where(lane == 16 * head + number, part, stats)
    return stats.astype(BF16)


def split3(x):
    high = x.astype(BF16).astype(F32)
    middle = (x - high).astype(BF16).astype(F32)
    return high, middle, (x - high - middle).astype(BF16).astype(F32)


def step_kernel(first, prefill, decode, last, hops, meta, *refs):
    refs = list(refs)
    pieces = [refs.pop(0) for _ in hops]
    pq = refs.pop(0) if prefill else None
    dq = refs.pop(0) if decode else None
    if first:
        acc_in = c_in = None
    else:
        acc_in, c_in = refs.pop(0), refs.pop(0)
    if last:
        out_p = refs.pop(0) if prefill else None
        out_d = refs.pop(0) if decode else None
        acc_out = c_out = None
    else:
        acc_out, c_out = refs.pop(0), refs.pop(0)
    qs = refs.pop(0)
    vts = [refs.pop(0) for _ in pieces]
    if last:
        acc_out, c_out = refs.pop(0), refs.pop(0)
    if first:
        acc_in, c_in = refs.pop(0), refs.pop(0)
    decode_tile = acc_in.shape[0] - 1
    begin = 0 if prefill else decode_tile
    end = decode_tile + 1 if decode else decode_tile
    heads = range(begin, decode_tile)

    seq, own_tp = meta[0], meta[1]
    z, core = seq >> 1, seq & 1
    open_to_prefix = [core > 0 if hop == 0 else ((z - hop + 2 * hop * core) & 7) < z for hop in hops]

    for head in heads:
        qs[head] = pq[:, head * HEAD_DIM : (head + 1) * HEAD_DIM]
    if decode:
        rows = dq.shape[0]
        for head in range(GROUP):
            qs[decode_tile, head * rows : (head + 1) * rows, :] = dq[:, head * HEAD_DIM : (head + 1) * HEAD_DIM]
    for piece, vt in zip(pieces, vts):
        for half in range(piece.shape[0]):
            for tile in range(4):
                at = (half * 4 + tile) * 128
                vt[0:HEAD_DIM, at : at + 128] = piece[half, 1, tile * 128 : (tile + 1) * 128, :]
        vt[HEAD_DIM:EXT, :] = jnp.ones((EXT - HEAD_DIM, vt.shape[1]), BF16)

    def add(tile, number, init):
        piece, vt = pieces[number], vts[number]
        parts = [
            jnp.exp2(dot(piece[half, 0], qs[tile], NT) * SCALE - c_out[tile, 0:1, :]).astype(BF16)
            for half in range(piece.shape[0])
        ]
        weights = parts[0] if len(parts) == 1 else jnp.concatenate(parts, axis=0)
        return init + dot(vt[...], weights, NN)

    if first:
        shape = (512, 512)
        row = lax.broadcasted_iota(jnp.int32, shape, 0)
        column = lax.broadcasted_iota(jnp.int32, shape, 1)
        position = jnp.where(row < 256, row + 256 * own_tp, row - 256 * own_tp)
        allowed = position <= column
        for tile in range(begin, end):
            scores = dot(pieces[0][0, 0], qs[tile], NT) * SCALE
            if tile in heads:
                scores = jnp.where(allowed, scores, NEGATIVE)
            peak = jnp.max(scores, axis=0, keepdims=True)
            acc_in[tile] = dot(vts[0][...], jnp.exp2(scores - peak).astype(BF16), NN)
            c_in[tile] = jnp.broadcast_to(peak, c_in.shape[1:])
    rest = range(1 if first else 0, len(hops))

    acc_out[begin:end] = acc_in[begin:end]
    c_out[begin:end] = c_in[begin:end]
    for number in rest:
        if prefill:

            @pl.when(open_to_prefix[number])
            def _():
                for tile in range(begin, end):
                    acc_out[tile] = add(tile, number, acc_out[tile])

        if decode:

            @pl.when(jnp.logical_not(open_to_prefix[number]) if prefill else number >= 0)
            def _():
                acc_out[decode_tile] = add(decode_tile, number, acc_out[decode_tile])

    top = jnp.max(acc_out[begin:end, HEAD_DIM : HEAD_DIM + 1, :])

    @pl.when(jnp.logical_not(top < LARGE))
    def _():
        def online(tile, number):
            piece, vt = pieces[number], vts[number]

            def some(part, carry):
                keys = piece[part // 4, 0, pl.ds(pl.multiple_of(part % 4 * 128, 128), 128), :]
                scores = dot(keys, qs[tile], NT) * SCALE
                before = c_out[tile, 0:1, :]
                peak = jnp.maximum(before, jnp.max(scores, axis=0, keepdims=True))
                values = vt[:, pl.ds(pl.multiple_of(part * 128, 128), 128)]
                update = dot(values, jnp.exp2(scores - peak).astype(BF16), NN)
                acc_out[tile] = acc_out[tile] * jnp.exp2(before - peak) + update
                c_out[tile] = jnp.broadcast_to(peak, c_out.shape[1:])
                return carry

            lax.fori_loop(0, vt.shape[1] // 128, some, 0)

        def again(tile, carry):
            acc_out[tile] = acc_in[tile]
            c_out[tile] = c_in[tile]
            for number in rest:

                @pl.when(jnp.logical_or(tile == decode_tile, open_to_prefix[number]))
                def _():
                    online(tile, number)

            return carry

        lax.fori_loop(begin, end, again, 0)

    if last and prefill:
        for head in heads:
            totals = acc_out[head, HEAD_DIM : HEAD_DIM + 1, :]
            result = (acc_out[head, 0:HEAD_DIM, :] * (1.0 / totals)).astype(BF16)
            out_p[:, head * HEAD_DIM : (head + 1) * HEAD_DIM] = result.T
    if last and decode:
        totals = acc_out[decode_tile, HEAD_DIM : HEAD_DIM + 1, :]
        result = (acc_out[decode_tile, 0:HEAD_DIM, :] * (1.0 / totals)).astype(BF16).T
        rows = dq.shape[0]
        stats = list(split3(c_out[decode_tile, 0:1, :])) + list(split3(totals))
        stats.append(jnp.zeros((16 - len(stats), GROUP * rows), F32))
        table = jnp.concatenate([jnp.concatenate(stats, axis=0)] * GROUP, axis=0)
        slot = lax.broadcasted_iota(jnp.int32, table.shape, 0)
        column = lax.broadcasted_iota(jnp.int32, table.shape, 1)
        table = jnp.where(slot // 16 == column // rows, table, 0.0).astype(BF16).T.astype(F32)
        packed = jnp.zeros((rows, HEAD_DIM), F32)
        for head in range(GROUP):
            out_d[:, head * HEAD_DIM : (head + 1) * HEAD_DIM] = result[head * rows : (head + 1) * rows, :]
            packed = packed + table[head * rows : (head + 1) * rows, :]
        out_d[:, GROUP * HEAD_DIM :] = packed.astype(BF16)


def step(meta, pieces, hops, pq, dq, state, last=False):
    first = state is None
    prefill, decode = pq is not None, dq is not None
    queries = 512
    tiles = 5 if first else state[0].shape[0]
    widths = [512 * piece.shape[0] for piece in pieces]
    acc = (tiles, EXT, queries)
    cs = (tiles, 8, queries)
    args = [meta] + list(pieces) + [x for x in (pq, dq) if x is not None]
    if not first:
        args += list(state)
    if last:
        out_shape = []
        if prefill:
            out_shape.append(jax.ShapeDtypeStruct(pq.shape, BF16))
        if decode:
            out_shape.append(jax.ShapeDtypeStruct((dq.shape[0], dq.shape[1] + 128), BF16))
    else:
        out_shape = [jax.ShapeDtypeStruct(acc, F32), jax.ShapeDtypeStruct(cs, F32)]
    scratch = [pltpu.VMEM((tiles, queries, HEAD_DIM), BF16)]
    scratch += [pltpu.VMEM((EXT, width), BF16) for width in widths]
    if last or first:
        scratch += [pltpu.VMEM(acc, F32), pltpu.VMEM(cs, F32)]
    used = 4 * prefill + decode
    flops = 4 * HEAD_DIM * used * queries * sum(widths)
    return pl.pallas_call(
        functools.partial(step_kernel, first, prefill, decode, last, tuple(hops)),
        out_shape=out_shape,
        in_specs=[SM] + [VM] * (len(args) - 1),
        out_specs=[VM] * len(out_shape),
        scratch_shapes=scratch,
        compiler_params=pltpu.CompilerParams(vmem_limit_bytes=LIMIT),
        cost_estimate=pl.CostEstimate(
            flops=2 * flops, bytes_accessed=4 * 2**20, transcendentals=used * queries * sum(widths)
        ),
        name="step",
    )(*args)


def suffix_kernel(
    begin, lengths, query, key_hbm, value_hbm, step_key, step_value, sums, stats, cache_key, cache_value, arrived
):
    rows, positions, lanes_all = cache_key.shape
    copies = []
    chunk = lanes_all // CHUNKS
    for number in range(CHUNKS):
        at = slice(number * chunk, (number + 1) * chunk)
        there = slice(begin * HEAD_DIM + number * chunk, begin * HEAD_DIM + (number + 1) * chunk)
        for which, (source, target) in enumerate(((key_hbm, cache_key), (value_hbm, cache_value))):
            copies.append(
                pltpu.make_async_copy(source.at[:, :, there], target.at[:, :, at], arrived.at[2 * number + which])
            )
    for copy in copies[:4]:
        copy.start()
    count = rows * STEPS
    shape = (GROUP * count, positions)
    place = lax.broadcasted_iota(jnp.int32, shape, 0) % count
    key_pos = lax.broadcasted_iota(jnp.int32, shape, 1)
    cached = [jnp.logical_and(place // STEPS == row, key_pos < lengths[row]) for row in range(rows)]
    shape = (GROUP * count, 128)
    place = lax.broadcasted_iota(jnp.int32, shape, 0) % count
    fresh = lax.broadcasted_iota(jnp.int32, shape, 1)
    recent = jnp.logical_and(place // STEPS == fresh // STEPS, fresh <= place)
    blank = jnp.zeros((128 - count, HEAD_DIM), F32)

    heads = sums.shape[0]
    for kv in range(heads):
        lanes = slice(kv * HEAD_DIM, (kv + 1) * HEAD_DIM)
        fresh_lanes = slice((begin + kv) * HEAD_DIM, (begin + kv + 1) * HEAD_DIM)
        if kv % (heads // CHUNKS) == 0:
            first = 2 * (kv // (heads // CHUNKS))
            copies[first].wait()
            copies[first + 1].wait()
            for copy in copies[first + 4 : first + 6]:
                copy.start()
        queries = jnp.concatenate(
            [query[begin + kv, :, head * HEAD_DIM : (head + 1) * HEAD_DIM].astype(F32) for head in range(GROUP)], axis=0
        ).astype(BF16)

        def filled(array):
            return jnp.concatenate(
                [array[row, :, fresh_lanes].astype(F32) for row in range(rows)] + [blank], axis=0
            ).astype(BF16)

        scores = [
            jnp.where(cached[row], dot(queries, cache_key[row, :, lanes], NT) * SCALE, NEGATIVE)
            for row in range(rows)
        ]
        scores.append(jnp.where(recent, dot(queries, filled(step_key), NT) * SCALE, NEGATIVE))
        peak = functools.reduce(jnp.maximum, [jnp.max(part, axis=1, keepdims=True) for part in scores])
        weights = [jnp.exp2(part - peak) for part in scores]
        total = functools.reduce(jnp.add, [jnp.sum(part, axis=1, keepdims=True) for part in weights])
        values = [cache_value[row, :, lanes] for row in range(rows)] + [filled(step_value)]
        result = dot(weights[0].astype(BF16), values[0], NN)
        for part, value in zip(weights[1:], values[1:]):
            result = result + dot(part.astype(BF16), value, NN)
        for head in range(GROUP):
            sums[kv, :, head * HEAD_DIM : (head + 1) * HEAD_DIM] = result[head * count : (head + 1) * count, :]
        stats[kv] = stat_lanes(peak, total, count)


def suffix(begin, heads, lengths, query, cache_key, cache_value, step_key, step_value):
    count = query.shape[1]
    held = cache_key.shape[:2] + (heads * HEAD_DIM,)
    return pl.pallas_call(
        functools.partial(suffix_kernel, begin),
        out_shape=[
            jax.ShapeDtypeStruct((heads,) + query.shape[1:], F32),
            jax.ShapeDtypeStruct((heads, count, 128), BF16),
        ],
        in_specs=[SM, VM, HBM, HBM, VM, VM],
        out_specs=[VM] * 2,
        scratch_shapes=[
            pltpu.VMEM(held, BF16),
            pltpu.VMEM(held, BF16),
            pltpu.SemaphoreType.DMA((2 * CHUNKS,)),
        ],
        compiler_params=pltpu.CompilerParams(vmem_limit_bytes=60 * 2**20),
        cost_estimate=pl.CostEstimate(flops=2 * 10**9, bytes_accessed=3 * 2**20, transcendentals=10**6),
        name="suffix",
    )(lengths, query, cache_key, cache_value, step_key, step_value)


def merge_kernel(prefix, sums_low, stats_low, sums_high, stats_high, out):
    width = GROUP * HEAD_DIM
    slot = lax.broadcasted_iota(jnp.int32, (128, width), 0)
    head = lax.broadcasted_iota(jnp.int32, (128, width), 1) // HEAD_DIM
    pick_c = jnp.where(jnp.logical_and(slot // 16 == head, slot % 16 < 3), 1.0, 0.0).astype(BF16)
    pick_total = jnp.where(
        jnp.logical_and(slot // 16 == head, jnp.logical_and(slot % 16 >= 3, slot % 16 < 6)), 1.0, 0.0
    ).astype(BF16)
    count = prefix.shape[1]
    early = jnp.concatenate([prefix[kv, :, width:].astype(F32) for kv in range(KV_HEADS)], axis=0).astype(BF16)
    half = sums_low.shape[0]
    sums = [sums_low[kv] for kv in range(half)] + [sums_high[kv] for kv in range(half)]
    stats = [stats_low[kv] for kv in range(half)] + [stats_high[kv] for kv in range(half)]
    late = jnp.concatenate([stat.astype(F32) for stat in stats], axis=0).astype(BF16)
    c, total = dot(early, pick_c, NN), dot(early, pick_total, NN)
    peak, late_total = dot(late, pick_c, NN), dot(late, pick_total, NN)
    top = jnp.maximum(peak, c)
    prior = jnp.exp2(c - top) * total
    later = jnp.exp2(peak - top)
    scale = 1.0 / (prior + late_total * later)
    prior, later = prior * scale, later * scale
    for kv in range(KV_HEADS):
        rows = slice(kv * count, (kv + 1) * count)
        mixed = prefix[kv, :, 0:width].astype(F32) * prior[rows] + sums[kv] * later[rows]
        for row in range(out.shape[0]):
            out[row, :, kv * width : (kv + 1) * width] = mixed[row * STEPS : (row + 1) * STEPS].astype(BF16)


def local(
    prefix_query,
    prefix_key,
    prefix_value,
    step_query,
    cache_key,
    cache_value,
    step_key,
    step_value,
    suffix_lengths,
):
    meta = jnp.stack([lax.axis_index("seq"), lax.axis_index("tp")])
    seq_count = 16

    def swap_cores(x):
        return lax.ppermute(x, "seq", [(i, i ^ 1) for i in range(seq_count)])

    def along_ring(x):
        return lax.ppermute(
            x, "seq", [(i, (i + (2 if i % 2 == 0 else -2)) % seq_count) for i in range(seq_count)]
        )

    def over_groups(x):
        return lax.all_to_all(x, "grp", split_axis=0, concat_axis=0, tiled=True)

    count = step_query.shape[0] * STEPS
    width = GROUP * HEAD_DIM
    own, parts = pl.pallas_call(
        pack_kernel,
        out_shape=[
            jax.ShapeDtypeStruct((2,) + prefix_key.shape, BF16),
            jax.ShapeDtypeStruct((KV_HEADS, count, width), BF16),
        ],
        in_specs=[VM] * 3,
        out_specs=[VM] * 2,
        compiler_params=pltpu.CompilerParams(vmem_limit_bytes=60 * 2**20),
        name="pack",
    )(prefix_key, prefix_value, step_query)
    other = lax.ppermute(own, "tp", [(0, 1), (1, 0)])
    own_rows = (suffix_lengths, parts, cache_key, cache_value, step_key, step_value)
    half = KV_HEADS // 2
    low = suffix(0, half, *own_rows)
    other, low = lax.optimization_barrier((other, low))

    mine = jnp.concatenate([own, other], axis=1)[None]
    theirs = swap_cores(mine)
    block = jnp.concatenate([mine, theirs], axis=0)

    coming = along_ring(block)
    parts, block = lax.optimization_barrier((parts, block))
    routed = over_groups(parts)
    high = suffix(half, half, suffix_lengths, parts, *own_rows[2:])
    routed, high = lax.optimization_barrier((routed, high))
    routed = routed.reshape(KV_HEADS * count, width)
    block = coming
    coming = along_ring(block)
    state = step(meta, [mine, theirs, block], [0, 0, 1], prefix_query, routed, None)
    block, state = lax.optimization_barrier((block, state))
    across = swap_cores(block)
    for hop in range(2, 4):
        before = across
        block, state = lax.optimization_barrier((coming, state))
        coming = along_ring(block)
        across = swap_cores(block) if hop == 3 else None
        state = step(meta, [before, block], [1 - hop, hop], prefix_query, routed, state)
        if across is None:
            block, state = lax.optimization_barrier((block, state))
            across = swap_cores(block)
    before, state = lax.optimization_barrier((across, state))
    state = step(meta, [before], [-3], prefix_query, routed, state)
    block, state = lax.optimization_barrier((coming, state))
    (partial,) = step(meta, [block], [4], None, routed, state, last=True)
    back = over_groups(partial.reshape(KV_HEADS, count, -1))
    (prefix_output,) = step(meta, [block], [4], prefix_query, None, state, last=True)
    step_output = pl.pallas_call(
        merge_kernel,
        out_shape=jax.ShapeDtypeStruct(step_query.shape, BF16),
        in_specs=[VM] * 5,
        out_specs=VM,
        compiler_params=pltpu.CompilerParams(vmem_limit_bytes=24 * 2**20),
        name="merge",
    )(back, *low, *high)
    return prefix_output, step_output


def solution(mesh):
    rows = P(("seq", "grp", "tp"), None, None)
    return jax.shard_map(
        local,
        mesh=mesh,
        in_specs=(
            P("seq", ("grp", "tp")),
            P(("seq", "tp"), "grp"),
            P(("seq", "tp"), "grp"),
            rows,
            rows,
            rows,
            rows,
            rows,
            P(("seq", "grp", "tp")),
        ),
        out_specs=(P("seq", ("grp", "tp")), rows),
        check_vma=False,
    )
```

```python
import functools

import jax
import jax.numpy as jnp
from jax import lax
from jax.experimental import pallas as pl
from jax.experimental.pallas import tpu as pltpu
from jax.sharding import PartitionSpec as P

HEADS = 64
KV_HEADS = 8
HEAD_DIM = 128
STEPS = 4
GROUP = HEADS // KV_HEADS

F32 = jnp.float32
BF16 = jnp.bfloat16
NEGATIVE = -1e30
SCALE = HEAD_DIM**-0.5 * 1.4426950408889634
LARGE = 2.0**100
NT = (((1,), (1,)), ((), ()))
NN = (((1,), (0,)), ((), ()))
EXT = HEAD_DIM + 16
LIMIT = 36 * 2**20
VM = pl.BlockSpec(memory_space=pltpu.VMEM)
SM = pl.BlockSpec(memory_space=pltpu.SMEM)
HBM = pl.BlockSpec(memory_space=pltpu.HBM)
CHUNKS = 2


def dot(a, b, dims):
    return lax.dot_general(a, b, dims, preferred_element_type=F32)


def pack_kernel(key, value, query, out, parts):
    out[0] = key[...]
    for tile in range(value.shape[0] // 128):
        rows = slice(tile * 128, (tile + 1) * 128)
        out[1, rows, :] = value[rows, :].astype(F32).T.astype(BF16)
    width = parts.shape[2]
    for kv in range(KV_HEADS):
        lanes = slice(kv * width, (kv + 1) * width)
        parts[kv] = jnp.concatenate(
            [query[row, :, lanes].astype(F32) for row in range(query.shape[0])], axis=0
        ).astype(BF16)


def stat_lanes(peak, total, count):
    lane = lax.broadcasted_iota(jnp.int32, (count, 128), 1)
    stats = jnp.zeros((count, 128), F32)
    for head in range(GROUP):
        here = slice(head * count, (head + 1) * count)
        for number, part in enumerate(split3(peak[here]) + split3(total[here])):
            stats = jnp.where(lane == 16 * head + number, part, stats)
    return stats.astype(BF16)


def split3(x):
    high = x.astype(BF16).astype(F32)
    middle = (x - high).astype(BF16).astype(F32)
    return high, middle, (x - high - middle).astype(BF16).astype(F32)


def step_kernel(first, prefill, decode, last, hops, meta, *refs):
    refs = list(refs)
    pieces = [refs.pop(0) for _ in hops]
    pq = refs.pop(0) if prefill else None
    dq = refs.pop(0) if decode else None
    if first:
        acc_in = c_in = None
    else:
        acc_in, c_in = refs.pop(0), refs.pop(0)
    if last:
        out_p = refs.pop(0) if prefill else None
        out_d = refs.pop(0) if decode else None
        acc_out = c_out = None
    else:
        acc_out, c_out = refs.pop(0), refs.pop(0)
    qs = refs.pop(0)
    vts = [refs.pop(0) for _ in pieces]
    if last:
        acc_out, c_out = refs.pop(0), refs.pop(0)
    if first:
        acc_in, c_in = refs.pop(0), refs.pop(0)
    decode_tile = acc_in.shape[0] - 1
    begin = 0 if prefill else decode_tile
    end = decode_tile + 1 if decode else decode_tile
    heads = range(begin, decode_tile)

    seq, own_tp = meta[0], meta[1]
    z, core = seq >> 1, seq & 1
    open_to_prefix = [core > 0 if hop == 0 else ((z - hop + 2 * hop * core) & 7) < z for hop in hops]

    for head in heads:
        qs[head] = pq[:, head * HEAD_DIM : (head + 1) * HEAD_DIM]
    if decode:
        rows = dq.shape[0]
        for head in range(GROUP):
            qs[decode_tile, head * rows : (head + 1) * rows, :] = dq[:, head * HEAD_DIM : (head + 1) * HEAD_DIM]
    for piece, vt in zip(pieces, vts):
        for half in range(piece.shape[0]):
            for tile in range(4):
                at = (half * 4 + tile) * 128
                vt[0:HEAD_DIM, at : at + 128] = piece[half, 1, tile * 128 : (tile + 1) * 128, :]
        vt[HEAD_DIM:EXT, :] = jnp.ones((EXT - HEAD_DIM, vt.shape[1]), BF16)

    def add(tile, number, init):
        piece, vt = pieces[number], vts[number]
        parts = [
            jnp.exp2(dot(piece[half, 0], qs[tile], NT) * SCALE - c_out[tile, 0:1, :]).astype(BF16)
            for half in range(piece.shape[0])
        ]
        weights = parts[0] if len(parts) == 1 else jnp.concatenate(parts, axis=0)
        return init + dot(vt[...], weights, NN)

    if first:
        shape = (512, 512)
        row = lax.broadcasted_iota(jnp.int32, shape, 0)
        column = lax.broadcasted_iota(jnp.int32, shape, 1)
        position = jnp.where(row < 256, row + 256 * own_tp, row - 256 * own_tp)
        allowed = position <= column
        for tile in range(begin, end):
            scores = dot(pieces[0][0, 0], qs[tile], NT) * SCALE
            if tile in heads:
                scores = jnp.where(allowed, scores, NEGATIVE)
            peak = jnp.max(scores, axis=0, keepdims=True)
            acc_in[tile] = dot(vts[0][...], jnp.exp2(scores - peak).astype(BF16), NN)
            c_in[tile] = jnp.broadcast_to(peak, c_in.shape[1:])
    rest = range(1 if first else 0, len(hops))

    c_out[begin:end] = c_in[begin:end]
    for number in rest:
        source = acc_in if number == rest[0] else acc_out
        if prefill:

            @pl.when(open_to_prefix[number])
            def _():
                for tile in range(begin, end):
                    acc_out[tile] = add(tile, number, source[tile])

        @pl.when(jnp.logical_not(open_to_prefix[number]) if prefill else number >= 0)
        def _():
            if decode:
                acc_out[decode_tile] = add(decode_tile, number, source[decode_tile])
            if prefill and number == rest[0]:
                acc_out[begin:decode_tile] = acc_in[begin:decode_tile]

    top = jnp.max(acc_out[begin:end, HEAD_DIM : HEAD_DIM + 1, :])

    @pl.when(jnp.logical_not(top < LARGE))
    def _():
        def online(tile, number):
            piece, vt = pieces[number], vts[number]

            def some(part, carry):
                keys = piece[part // 4, 0, pl.ds(pl.multiple_of(part % 4 * 128, 128), 128), :]
                scores = dot(keys, qs[tile], NT) * SCALE
                before = c_out[tile, 0:1, :]
                peak = jnp.maximum(before, jnp.max(scores, axis=0, keepdims=True))
                values = vt[:, pl.ds(pl.multiple_of(part * 128, 128), 128)]
                update = dot(values, jnp.exp2(scores - peak).astype(BF16), NN)
                acc_out[tile] = acc_out[tile] * jnp.exp2(before - peak) + update
                c_out[tile] = jnp.broadcast_to(peak, c_out.shape[1:])
                return carry

            lax.fori_loop(0, vt.shape[1] // 128, some, 0)

        def again(tile, carry):
            acc_out[tile] = acc_in[tile]
            c_out[tile] = c_in[tile]
            for number in rest:

                @pl.when(jnp.logical_or(tile == decode_tile, open_to_prefix[number]))
                def _():
                    online(tile, number)

            return carry

        lax.fori_loop(begin, end, again, 0)

    if last and prefill:
        for head in heads:
            totals = acc_out[head, HEAD_DIM : HEAD_DIM + 1, :]
            result = (acc_out[head, 0:HEAD_DIM, :] * (1.0 / totals)).astype(BF16)
            out_p[:, head * HEAD_DIM : (head + 1) * HEAD_DIM] = result.T
    if last and decode:
        totals = acc_out[decode_tile, HEAD_DIM : HEAD_DIM + 1, :]
        result = (acc_out[decode_tile, 0:HEAD_DIM, :] * (1.0 / totals)).astype(BF16).T
        rows = dq.shape[0]
        stats = list(split3(c_out[decode_tile, 0:1, :])) + list(split3(totals))
        stats.append(jnp.zeros((16 - len(stats), GROUP * rows), F32))
        table = jnp.concatenate([jnp.concatenate(stats, axis=0)] * GROUP, axis=0)
        slot = lax.broadcasted_iota(jnp.int32, table.shape, 0)
        column = lax.broadcasted_iota(jnp.int32, table.shape, 1)
        table = jnp.where(slot // 16 == column // rows, table, 0.0).astype(BF16).T.astype(F32)
        packed = jnp.zeros((rows, HEAD_DIM), F32)
        for head in range(GROUP):
            out_d[:, head * HEAD_DIM : (head + 1) * HEAD_DIM] = result[head * rows : (head + 1) * rows, :]
            packed = packed + table[head * rows : (head + 1) * rows, :]
        out_d[:, GROUP * HEAD_DIM :] = packed.astype(BF16)


def step(meta, pieces, hops, pq, dq, state, last=False):
    first = state is None
    prefill, decode = pq is not None, dq is not None
    queries = 512
    tiles = 5 if first else state[0].shape[0]
    widths = [512 * piece.shape[0] for piece in pieces]
    acc = (tiles, EXT, queries)
    cs = (tiles, 8, queries)
    args = [meta] + list(pieces) + [x for x in (pq, dq) if x is not None]
    if not first:
        args += list(state)
    if last:
        out_shape = []
        if prefill:
            out_shape.append(jax.ShapeDtypeStruct(pq.shape, BF16))
        if decode:
            out_shape.append(jax.ShapeDtypeStruct((dq.shape[0], dq.shape[1] + 128), BF16))
    else:
        out_shape = [jax.ShapeDtypeStruct(acc, F32), jax.ShapeDtypeStruct(cs, F32)]
    scratch = [pltpu.VMEM((tiles, queries, HEAD_DIM), BF16)]
    scratch += [pltpu.VMEM((EXT, width), BF16) for width in widths]
    if last or first:
        scratch += [pltpu.VMEM(acc, F32), pltpu.VMEM(cs, F32)]
    used = 4 * prefill + decode
    flops = 4 * HEAD_DIM * used * queries * sum(widths)
    return pl.pallas_call(
        functools.partial(step_kernel, first, prefill, decode, last, tuple(hops)),
        out_shape=out_shape,
        in_specs=[SM] + [VM] * (len(args) - 1),
        out_specs=[VM] * len(out_shape),
        scratch_shapes=scratch,
        compiler_params=pltpu.CompilerParams(vmem_limit_bytes=LIMIT),
        cost_estimate=pl.CostEstimate(
            flops=2 * flops, bytes_accessed=4 * 2**20, transcendentals=used * queries * sum(widths)
        ),
        name="step",
    )(*args)


def suffix_kernel(
    begin, lengths, query_hbm, key_hbm, value_hbm, step_key_hbm, step_value_hbm, sums, stats,
    cache_key, cache_value, query, step_key, step_value, arrived, ready
):
    rows, positions, lanes_all = cache_key.shape
    copies = []
    chunk = lanes_all // CHUNKS
    for number in range(CHUNKS):
        at = slice(number * chunk, (number + 1) * chunk)
        there = slice(begin * HEAD_DIM + number * chunk, begin * HEAD_DIM + (number + 1) * chunk)
        for which, (source, target) in enumerate(((key_hbm, cache_key), (value_hbm, cache_value))):
            copies.append(
                pltpu.make_async_copy(source.at[:, :, there], target.at[:, :, at], arrived.at[2 * number + which])
            )
    small = [
        pltpu.make_async_copy(source, target, ready.at[number])
        for number, (source, target) in enumerate(
            ((query_hbm, query), (step_key_hbm, step_key), (step_value_hbm, step_value))
        )
    ]
    for copy in small + copies[:4]:
        copy.start()
    for copy in small:
        copy.wait()
    count = rows * STEPS
    shape = (GROUP * count, positions)
    place = lax.broadcasted_iota(jnp.int32, shape, 0) % count
    key_pos = lax.broadcasted_iota(jnp.int32, shape, 1)
    cached = [jnp.logical_and(place // STEPS == row, key_pos < lengths[row]) for row in range(rows)]
    shape = (GROUP * count, 128)
    place = lax.broadcasted_iota(jnp.int32, shape, 0) % count
    fresh = lax.broadcasted_iota(jnp.int32, shape, 1)
    recent = jnp.logical_and(place // STEPS == fresh // STEPS, fresh <= place)
    blank = jnp.zeros((128 - count, HEAD_DIM), F32)

    heads = sums.shape[0]
    for kv in range(heads):
        lanes = slice(kv * HEAD_DIM, (kv + 1) * HEAD_DIM)
        fresh_lanes = slice((begin + kv) * HEAD_DIM, (begin + kv + 1) * HEAD_DIM)
        if kv % (heads // CHUNKS) == 0:
            first = 2 * (kv // (heads // CHUNKS))
            copies[first].wait()
            copies[first + 1].wait()
            for copy in copies[first + 4 : first + 6]:
                copy.start()
        queries = jnp.concatenate(
            [query[begin + kv, :, head * HEAD_DIM : (head + 1) * HEAD_DIM].astype(F32) for head in range(GROUP)], axis=0
        ).astype(BF16)

        def filled(array):
            return jnp.concatenate(
                [array[row, :, fresh_lanes].astype(F32) for row in range(rows)] + [blank], axis=0
            ).astype(BF16)

        scores = [
            jnp.where(cached[row], dot(queries, cache_key[row, :, lanes], NT) * SCALE, NEGATIVE)
            for row in range(rows)
        ]
        scores.append(jnp.where(recent, dot(queries, filled(step_key), NT) * SCALE, NEGATIVE))
        peak = functools.reduce(jnp.maximum, [jnp.max(part, axis=1, keepdims=True) for part in scores])
        weights = [jnp.exp2(part - peak) for part in scores]
        total = functools.reduce(jnp.add, [jnp.sum(part, axis=1, keepdims=True) for part in weights])
        values = [cache_value[row, :, lanes] for row in range(rows)] + [filled(step_value)]
        result = dot(weights[0].astype(BF16), values[0], NN)
        for part, value in zip(weights[1:], values[1:]):
            result = result + dot(part.astype(BF16), value, NN)
        for head in range(GROUP):
            sums[kv, :, head * HEAD_DIM : (head + 1) * HEAD_DIM] = result[head * count : (head + 1) * count, :]
        stats[kv] = stat_lanes(peak, total, count)


def suffix(begin, heads, lengths, query, cache_key, cache_value, step_key, step_value):
    count = query.shape[1]
    held = cache_key.shape[:2] + (heads * HEAD_DIM,)
    return pl.pallas_call(
        functools.partial(suffix_kernel, begin),
        out_shape=[
            jax.ShapeDtypeStruct((heads,) + query.shape[1:], F32),
            jax.ShapeDtypeStruct((heads, count, 128), BF16),
        ],
        in_specs=[SM] + [HBM] * 5,
        out_specs=[VM] * 2,
        scratch_shapes=[
            pltpu.VMEM(held, BF16),
            pltpu.VMEM(held, BF16),
            pltpu.VMEM(query.shape, BF16),
            pltpu.VMEM(step_key.shape, BF16),
            pltpu.VMEM(step_value.shape, BF16),
            pltpu.SemaphoreType.DMA((2 * CHUNKS,)),
            pltpu.SemaphoreType.DMA((3,)),
        ],
        compiler_params=pltpu.CompilerParams(vmem_limit_bytes=60 * 2**20),
        cost_estimate=pl.CostEstimate(flops=2 * 10**9, bytes_accessed=3 * 2**20, transcendentals=10**6),
        name="suffix",
    )(lengths, query, cache_key, cache_value, step_key, step_value)


def merge_kernel(prefix, sums_low, stats_low, sums_high, stats_high, out):
    width = GROUP * HEAD_DIM
    slot = lax.broadcasted_iota(jnp.int32, (128, width), 0)
    head = lax.broadcasted_iota(jnp.int32, (128, width), 1) // HEAD_DIM
    pick_c = jnp.where(jnp.logical_and(slot // 16 == head, slot % 16 < 3), 1.0, 0.0).astype(BF16)
    pick_total = jnp.where(
        jnp.logical_and(slot // 16 == head, jnp.logical_and(slot % 16 >= 3, slot % 16 < 6)), 1.0, 0.0
    ).astype(BF16)
    count = prefix.shape[1]
    early = jnp.concatenate([prefix[kv, :, width:].astype(F32) for kv in range(KV_HEADS)], axis=0).astype(BF16)
    half = sums_low.shape[0]
    sums = [sums_low[kv] for kv in range(half)] + [sums_high[kv] for kv in range(half)]
    stats = [stats_low[kv] for kv in range(half)] + [stats_high[kv] for kv in range(half)]
    late = jnp.concatenate([stat.astype(F32) for stat in stats], axis=0).astype(BF16)
    c, total = dot(early, pick_c, NN), dot(early, pick_total, NN)
    peak, late_total = dot(late, pick_c, NN), dot(late, pick_total, NN)
    top = jnp.maximum(peak, c)
    prior = jnp.exp2(c - top) * total
    later = jnp.exp2(peak - top)
    scale = 1.0 / (prior + late_total * later)
    prior, later = prior * scale, later * scale
    for kv in range(KV_HEADS):
        rows = slice(kv * count, (kv + 1) * count)
        mixed = prefix[kv, :, 0:width].astype(F32) * prior[rows] + sums[kv] * later[rows]
        for row in range(out.shape[0]):
            out[row, :, kv * width : (kv + 1) * width] = mixed[row * STEPS : (row + 1) * STEPS].astype(BF16)


def local(
    prefix_query,
    prefix_key,
    prefix_value,
    step_query,
    cache_key,
    cache_value,
    step_key,
    step_value,
    suffix_lengths,
):
    meta = jnp.stack([lax.axis_index("seq"), lax.axis_index("tp")])
    seq_count = 16

    def swap_cores(x):
        return lax.ppermute(x, "seq", [(i, i ^ 1) for i in range(seq_count)])

    def along_ring(x):
        return lax.ppermute(
            x, "seq", [(i, (i + (2 if i % 2 == 0 else -2)) % seq_count) for i in range(seq_count)]
        )

    def over_groups(x):
        return lax.all_to_all(x, "grp", split_axis=0, concat_axis=0, tiled=True)

    count = step_query.shape[0] * STEPS
    width = GROUP * HEAD_DIM
    own, parts = pl.pallas_call(
        pack_kernel,
        out_shape=[
            jax.ShapeDtypeStruct((2,) + prefix_key.shape, BF16),
            jax.ShapeDtypeStruct((KV_HEADS, count, width), BF16),
        ],
        in_specs=[VM] * 3,
        out_specs=[VM] * 2,
        compiler_params=pltpu.CompilerParams(vmem_limit_bytes=60 * 2**20),
        name="pack",
    )(prefix_key, prefix_value, step_query)
    other = lax.ppermute(own, "tp", [(0, 1), (1, 0)])
    own_rows = (suffix_lengths, parts, cache_key, cache_value, step_key, step_value)
    half = KV_HEADS // 2
    low = suffix(0, half, *own_rows)
    other, low = lax.optimization_barrier((other, low))

    mine = jnp.concatenate([own, other], axis=1)[None]
    theirs = swap_cores(mine)
    block = jnp.concatenate([mine, theirs], axis=0)

    coming = along_ring(block)
    parts, block = lax.optimization_barrier((parts, block))
    routed = over_groups(parts)
    high = suffix(half, half, suffix_lengths, parts, *own_rows[2:])
    routed, high = lax.optimization_barrier((routed, high))
    routed = routed.reshape(KV_HEADS * count, width)
    block = coming
    coming = along_ring(block)
    state = step(meta, [mine, theirs, block], [0, 0, 1], prefix_query, routed, None)
    block, state = lax.optimization_barrier((block, state))
    across = swap_cores(block)
    for hop in range(2, 4):
        before = across
        block, state = lax.optimization_barrier((coming, state))
        coming = along_ring(block)
        across = swap_cores(block) if hop == 3 else None
        pieces, hops = [before, block], [1 - hop, hop]
        if across is not None:
            pieces, hops = pieces + [across], hops + [-hop]
        state = step(meta, pieces, hops, prefix_query, routed, state)
        if across is None:
            block, state = lax.optimization_barrier((block, state))
            across = swap_cores(block)
    block, state = lax.optimization_barrier((coming, state))
    (partial,) = step(meta, [block], [4], None, routed, state, last=True)
    back = over_groups(partial.reshape(KV_HEADS, count, -1))
    (prefix_output,) = step(meta, [block], [4], prefix_query, None, state, last=True)
    step_output = pl.pallas_call(
        merge_kernel,
        out_shape=jax.ShapeDtypeStruct(step_query.shape, BF16),
        in_specs=[VM] * 5,
        out_specs=VM,
        compiler_params=pltpu.CompilerParams(vmem_limit_bytes=24 * 2**20),
        name="merge",
    )(back, *low, *high)
    return prefix_output, step_output


def solution(mesh):
    rows = P(("seq", "grp", "tp"), None, None)
    return jax.shard_map(
        local,
        mesh=mesh,
        in_specs=(
            P("seq", ("grp", "tp")),
            P(("seq", "tp"), "grp"),
            P(("seq", "tp"), "grp"),
            rows,
            rows,
            rows,
            rows,
            rows,
            P(("seq", "grp", "tp")),
        ),
        out_specs=(P("seq", ("grp", "tp")), rows),
        check_vma=False,
    )
```
